128 devices in a mesh: grp: 4 (over y), fsdp: 32 (over x, z, core).
Axes of the slice: x: 4, y: 4, z: 4, core: 2. Of those that a mesh axis runs over, the one named last changes fastest.
Arguments:
- tokens: bfloat16 [65536, 8192], P(('grp', 'fsdp')), may hold values from -6 to 6
- frozen_key_weight: bfloat16 [8192, 1024], P('fsdp'), may hold values from -0.0625 to 0.0625
- adapter_down: bfloat16 [8192, 512], replicated, may hold values from -0.0625 to 0.0625
- adapter_up: bfloat16 [1024, 512], replicated, may hold values from -0.75 to 0.75
- key_cotangent: bfloat16 [65536, 1024], P(('grp', 'fsdp')), may hold values from -24 to 24
- token_tasks: int32 [65536], P(('grp', 'fsdp')), may hold values from 0 to 7, never falling along the last dimension, each value on 1 to 16384 neighbouring positions
- owned: int32 [8], replicated, may hold values from 0 to 7, each once
- counts: int32 [8], replicated, may hold values from 32 to 128
Outputs:
- keys: bfloat16 [65536, 1024], P(('grp', 'fsdp'))
- grad_down: float32 [4, 8192, 128], P('grp', 'fsdp')
- grad_up: float32 [4, 1024, 128], P('grp', 'fsdp')
The draws below stay inside these ranges and needn't reach their ends.
Inputs may be any that keep to these rules, and one draw needn't show every extreme that they name: `token_tasks`: task ids never decrease along the tokens; every task has one token or more, and one task has exactly 16384. `owned`: every adapter appears once.
All inputs are finite; a program needn't handle non-finite values.
Results may differ from the reference program's by a relative error of at most 0.013.
Values may be sent and summed in bfloat16 or wider, within the bound.
No kernel may reach another device: no remote copies, remote signals or barrier semaphores. Data moves between devices by JAX's collectives and lax.ppermute only.
A program may use at most 192 MiB of HBM per device.

```python
import math
import jax
import jax.numpy as jnp
import numpy as np
from jax import lax

MODEL_WIDTH = 8192
KEY_WIDTH = 1024
ADAPTER_RANK = 64
ADP_GRP = 2
TOK_DEV = 512
TASK_ADAPTERS = 8
TOKENS = 65536
N_GRP = 4


def set_ends(values, key, smallest, top_value):
    longest = values.shape.index(max(values.shape))
    spots = []
    for shift in (0, 1):
        where = [jax.random.randint(jax.random.fold_in(key, axis), (), 0, length) for axis, length in enumerate(values.shape)]
        where[longest] = (where[longest] + shift) % values.shape[longest]
        spots.append(tuple(where))
    return values.at[spots[0]].set(smallest).at[spots[1]].set(top_value)


def with_spikes(values, key, source, target, shards_of, factor):
    owner, partner = [(jnp.arange(values.shape[axis_at]) // (values.shape[axis_at] // shards_of)).reshape([-1 if axis == axis_at else 1 for axis in range(values.ndim)]) for axis_at in (source, target)]
    chosen = jax.random.permutation(key, shards_of)[partner]
    strong = (owner == chosen) | (owner == (partner + shards_of // 2) % shards_of)
    return jnp.where(strong, factor * values, values)


def level_of(rng, extent, pieces, smallest, high):
    loudness, own = 1.0, jax.random.fold_in(rng, 6)
    for axis_at, shards_of in pieces:
        heights = jnp.exp(jax.random.uniform(jax.random.fold_in(own, axis_at), (shards_of,), jnp.float32, smallest / len(pieces), high / len(pieces)))
        loudness = loudness * jnp.repeat(heights, extent[axis_at] // shards_of).reshape([-1 if axis == axis_at else 1 for axis in range(len(extent))])
    return loudness


def split_up(amount, total, limit, slope):
    loads = [(1 << 20) // math.isqrt(grade ** slope) + 1 for grade in range(2, amount + 1)]
    spare, given = total - limit - (amount - 1), [1] * (amount - 1)
    while spare > 0:
        movable = [i for i in range(amount - 1) if given[i] < limit]
        mass, left = sum([loads[i] for i in movable]), spare
        for i in movable:
            extra = min(limit - given[i], max(1, left * loads[i] // mass), spare)
            given[i] = given[i] + extra
            spare = spare - extra
    return np.array([limit] + given)


def ragged_sizes(rng, count, total, bound, slope):
    if count == 2:
        one = jax.random.randint(rng, (), max(1, total - bound), min(bound, total - 1) + 1)
        return jnp.stack([one, total - one])
    lengths = jnp.asarray(split_up(count, total, bound, slope), jnp.int32)
    twos = (count - 1) // 2
    source_of, receiver = lengths[1:1 + 2 * twos:2], lengths[2:2 + 2 * twos:2]
    room = jnp.minimum(source_of - 1, bound - receiver)
    moved = jax.random.randint(jax.random.fold_in(rng, 1), (twos,), 0, 1 << 20) % (room + 1)
    lengths = lengths.at[1:1 + 2 * twos:2].set(source_of - moved).at[2:2 + 2 * twos:2].set(receiver + moved)
    return lengths[jax.random.permutation(jax.random.fold_in(rng, 2), count)]


def noise(own_key, dims, deviation, most, pieces=(), kind=jnp.bfloat16):
    array = jax.random.normal(own_key, dims, jnp.float32) * deviation
    if len(pieces) > 0:
        array = level_of(own_key, dims, pieces, -0.22, 0.18) * array
    return jnp.clip(array, min=-most, max=most).astype(kind)


def heavy_noise(own_key, shape, deviation, reach, shards, heavy, held_as=jnp.bfloat16):
    result = deviation * jax.random.normal(own_key, shape, jnp.float32)
    if shards:
        result = result * level_of(own_key, shape, shards, -0.22, 0.18)
    return jnp.clip(with_spikes(result, jax.random.fold_in(own_key, 3), *heavy), -reach, reach).astype(held_as)


def setup_inputs(seed: int = 0) -> dict:
    arg_keys = jax.random.split(jax.random.key(seed), 9)
    tokens = noise(arg_keys[0], (TOKENS, MODEL_WIDTH), 1.0, 6.0, ((0, 128),))
    frozen_key_weight = noise(arg_keys[1], (MODEL_WIDTH, KEY_WIDTH), MODEL_WIDTH ** -0.5, 0.0625, ((0, 32),))
    adapter_down = noise(arg_keys[2], (MODEL_WIDTH, TASK_ADAPTERS * ADAPTER_RANK), MODEL_WIDTH ** -0.5, 0.0625)
    adapter_up = noise(arg_keys[3], (KEY_WIDTH, TASK_ADAPTERS * ADAPTER_RANK), ADAPTER_RANK ** -0.5, 0.75)
    key_cotangent = heavy_noise(arg_keys[4], (TOKENS, KEY_WIDTH), 1.0, 24.0, ((0, 128),), (0, 1, 128, 5.5))
    token_tasks = jnp.searchsorted(jnp.cumsum(ragged_sizes(arg_keys[5], TASK_ADAPTERS, TOKENS, 2 * TOKENS // TASK_ADAPTERS, 2)), jnp.arange(TOKENS), side="right").astype(jnp.int32)
    owned = jax.random.permutation(arg_keys[6], TASK_ADAPTERS).astype(jnp.int32)
    counts = set_ends(jax.random.randint(arg_keys[7], (TASK_ADAPTERS,), 32, 129), jax.random.fold_in(arg_keys[7], 1), 32, 128).astype(jnp.int32)
    return {"tokens": tokens, "frozen_key_weight": frozen_key_weight, "adapter_down": adapter_down, "adapter_up": adapter_up, "key_cotangent": key_cotangent, "token_tasks": token_tasks, "owned": owned, "counts": counts}


ADAPTER_SCALE = 0.5


def owner_columns(owned, rank):
    return (owned[:, None] * rank + jnp.arange(rank, dtype=jnp.int32)[None, :]).reshape(-1)


def token_masks(token_tasks, owned, counts, rank):
    adapters = owned.shape[0]
    owner_hit = (token_tasks[:, None] == owned[None, :]).astype(jnp.float32)
    column_mask = jnp.repeat(owner_hit, rank, axis=1)
    task_hot = (token_tasks[:, None] == jnp.arange(adapters, dtype=jnp.int32)[None, :]).astype(jnp.float32)
    token_adapter_mask = jnp.sum(task_hot * counts.astype(jnp.float32)[None, :], axis=1)
    return column_mask, ADAPTER_SCALE / token_adapter_mask


def reference(tokens, frozen_key_weight, adapter_down, adapter_up, key_cotangent, token_tasks, owned, counts):
    column_position = owner_columns(owned, ADAPTER_RANK)
    down_selected = jnp.take(adapter_down, column_position, axis=1)
    up_selected = jnp.take(adapter_up, column_position, axis=1)
    blocks = TOKENS // TOK_DEV

    def step(carry, index):
        down_sum, up_sum = carry
        first = (index * TOK_DEV).astype(jnp.int32)
        block_tokens = lax.dynamic_slice_in_dim(tokens, first, TOK_DEV, 0)
        block_grad = lax.dynamic_slice_in_dim(key_cotangent, first, TOK_DEV, 0)
        block_tasks = lax.dynamic_slice_in_dim(token_tasks, first, TOK_DEV, 0)
        column_mask, token_weight = token_masks(block_tasks, owned, counts, ADAPTER_RANK)
        frozen_keys = jnp.dot(block_tokens, frozen_key_weight, preferred_element_type=jnp.float32)
        hidden = (jnp.dot(block_tokens, down_selected, preferred_element_type=jnp.float32) * column_mask).astype(jnp.bfloat16)
        adapted_keys = lax.dot_general(hidden, up_selected, (((1,), (1,)), ((), ())), preferred_element_type=jnp.float32)
        keys = (frozen_keys + ADAPTER_SCALE * adapted_keys).astype(jnp.bfloat16)
        scaled = (block_grad.astype(jnp.float32) * token_weight[:, None]).astype(jnp.bfloat16)
        up_term = lax.dot_general(scaled, hidden, (((0,), (0,)), ((), ())), preferred_element_type=jnp.float32)
        low_grad = (jnp.dot(scaled, up_selected, preferred_element_type=jnp.float32) * column_mask).astype(jnp.bfloat16)
        down_term = lax.dot_general(block_tokens, low_grad, (((0,), (0,)), ((), ())), preferred_element_type=jnp.float32)
        return (down_sum + down_term, up_sum + up_term), keys

    init = (jnp.zeros((MODEL_WIDTH, TASK_ADAPTERS * ADAPTER_RANK), jnp.float32), jnp.zeros((KEY_WIDTH, TASK_ADAPTERS * ADAPTER_RANK), jnp.float32))
    (down_sum, up_sum), keys = lax.scan(step, init, jnp.arange(blocks, dtype=jnp.int32))
    keys = keys.reshape(TOKENS, KEY_WIDTH)
    grad_down = jnp.transpose(down_sum.reshape(MODEL_WIDTH, N_GRP, ADP_GRP * ADAPTER_RANK), (1, 0, 2))
    grad_up = jnp.transpose(up_sum.reshape(KEY_WIDTH, N_GRP, ADP_GRP * ADAPTER_RANK), (1, 0, 2))
    return keys, grad_down, grad_up
```

```python
import jax
import jax.numpy as jnp
from jax import lax
from jax.sharding import Mesh, PartitionSpec as P

RANK = 64
SCALE = 0.5
BF = jnp.bfloat16
F32 = jnp.float32
SLOTS = 4
INFO = 16


def dot(a, b, dims=((1,), (0,))):
    return lax.dot_general(a, b, (dims, ((), ())), preferred_element_type=F32)


def exchange(a, axis):
    return lax.all_to_all(a, axis, 0, 0, tiled=True)


def info_rows(rows, width, flag):
    row = lax.broadcasted_iota(jnp.int32, (INFO, width), 0)
    return jnp.where(row == 0, rows[None, :], jnp.where(row == 1, flag, 0.0)).astype(BF)


def per_device(tokens, weight, down, up, cotangent, tasks, owned, counts):
    n_tok, width = tokens.shape
    kv = weight.shape[1]
    adapters = owned.shape[0]
    cols = adapters * RANK
    ny, nx, nz = lax.axis_size("y"), lax.axis_size("x"), lax.axis_size("z")
    me_c = lax.axis_index("c")
    d_rows, v_rows = width // (nx * nz * 2), kv // (nx * nz * 2)
    b_rows = d_rows + v_rows
    sc = SLOTS * RANK
    swap = [(0, 1), (1, 0)]

    full_weight = lax.all_gather(weight, ("x", "z", "c"), axis=0, tiled=True)

    ids = jnp.arange(adapters, dtype=jnp.int32)
    partner_tasks = lax.ppermute(tasks, "c", swap)
    hit = tasks[:, None] == ids[None, :]
    present = jnp.any(hit | (partner_tasks[:, None] == ids[None, :]), axis=0)
    rank_of = jnp.sum((ids[None, :] < ids[:, None]) & present[None, :], axis=1)
    col_slot = jnp.arange(sc, dtype=jnp.int32) // RANK
    col_rank = jnp.arange(sc, dtype=jnp.int32) % RANK
    chosen = present[None, :] & (rank_of[None, :] == col_slot[:, None])
    col_task = jnp.sum(jnp.where(chosen, ids[None, :] + 1, 0), axis=1) - 1
    overflow = (jnp.sum(present.astype(jnp.int32)) > SLOTS).astype(F32)

    row = jnp.arange(cols, dtype=jnp.int32)
    pick = ((row // RANK)[:, None] == col_task[None, :]) & ((row % RANK)[:, None] == col_rank[None, :])
    pick = pick.astype(BF)
    mask_full = (tasks[:, None] == (row // RANK)[None, :]).astype(F32)
    mask_slot = (tasks[:, None] == col_task[None, :]).astype(F32)

    token_count = jnp.sum(jnp.where(hit, counts.astype(F32)[None, :], 0.0), axis=1)
    scaled = (cotangent.astype(F32) * (SCALE / token_count)[:, None]).astype(BF)

    up_slot = dot(up, pick).astype(BF)
    low = (dot(scaled, up_slot) * mask_slot).astype(BF)
    hidden = (dot(tokens, down) * mask_full).astype(BF)
    hidden_slot = dot(hidden, pick).astype(BF)

    down_term = dot(tokens, low, ((0,), (0,))).reshape(nx, nz, 2, d_rows, sc)
    up_term = dot(scaled, hidden_slot, ((0,), (0,))).reshape(nx, nz, 2, v_rows, sc)
    term = jnp.concatenate([down_term, up_term], axis=3)
    theirs = lax.dynamic_index_in_dim(term, 1 - me_c, 2, keepdims=False).astype(BF)
    mine = lax.dynamic_index_in_dim(term, me_c, 2, keepdims=False)
    chip = (mine + lax.ppermute(theirs, "c", swap).astype(F32)).astype(BF)

    chip = jnp.transpose(chip, (1, 0, 2, 3)).reshape(nz, nx * b_rows, sc)
    note = jnp.broadcast_to(info_rows(col_task.astype(F32), sc, overflow)[None], (nz, INFO, sc))
    got = exchange(jnp.concatenate([chip, note], axis=1), "z")
    flag = jnp.max(got[:, nx * b_rows + 1, 0].astype(F32))
    sent_task = got[:, nx * b_rows, :].astype(F32)
    place = (sent_task[:, :, None] == owned[row // RANK].astype(F32)[None, None, :]) & (
        col_rank[None, :, None] == (row % RANK)[None, None, :]
    )
    spread = lax.dot_general(
        got[:, : nx * b_rows], place.astype(BF), (((2,), (1,)), ((0,), (0,))), preferred_element_type=F32
    ).sum(axis=0)

    own = cols // ny
    spread = jnp.transpose(spread.reshape(nx * b_rows, ny, own).astype(BF), (1, 0, 2))
    note = jnp.broadcast_to(info_rows(jnp.zeros((own,), F32), own, flag)[None], (ny, INFO, own))
    got = exchange(jnp.concatenate([spread, note], axis=1), "y").astype(F32)
    flag = jnp.max(got[:, nx * b_rows + 1, 0])
    part = got[:, : nx * b_rows].sum(axis=0).astype(BF).reshape(nx, b_rows, own)

    note = jnp.broadcast_to(info_rows(jnp.zeros((own,), F32), own, flag)[None], (nx, INFO, own))
    got = exchange(jnp.concatenate([part, note], axis=1), "x").astype(F32)
    flag = jnp.max(got[:, b_rows + 1, 0])
    total = got[:, :b_rows].sum(axis=0)
    grad_down, grad_up = total[:d_rows], total[d_rows:]

    keys = (dot(tokens, full_weight) + SCALE * dot(hidden, up, ((1,), (1,)))).astype(BF)

    flag, keys = lax.optimization_barrier((flag, keys))

    def rest(grads):
        left = (1.0 - jnp.sum(mask_slot, axis=1) / RANK)[:, None]
        order = ((row // RANK)[:, None] == owned[row // RANK][None, :]) & (
            (row % RANK)[:, None] == (row % RANK)[None, :]
        )
        order = order.astype(BF)
        low_left = (dot(scaled, up) * (mask_full * left)).astype(BF)
        low_left = dot(low_left, order).astype(BF)
        hid_left = dot((hidden * left).astype(BF), order).astype(BF)

        def summed(a, b):
            rows = a.shape[1]
            t = lax.dot_general(
                a, b.reshape(n_tok, ny, own), (((0,), (0,)), ((), ())), preferred_element_type=F32
            )
            t = jnp.transpose(t, (1, 0, 2)).reshape(ny * rows, own)
            for axis in ("y", "x", "z", "c"):
                t = lax.psum_scatter(t, axis, scatter_dimension=0, tiled=True)
            return t

        return grads[0] + summed(tokens, low_left), grads[1] + summed(scaled, hid_left)

    grad_down, grad_up = lax.cond(flag > 0.5, rest, lambda g: g, (grad_down, grad_up))
    return keys, grad_down[None], grad_up[None]


def solution(mesh):
    sizes = dict(mesh.shape)
    ny = sizes["grp"]
    nx = nz = int((sizes["fsdp"] // 2) ** 0.5)
    fine = Mesh(mesh.devices.reshape(ny, nx, nz, 2), ("y", "x", "z", "c"))
    fsdp = ("x", "z", "c")
    every = ("y", "x", "z", "c")
    in_specs = (P(every, None), P(fsdp, None), P(), P(), P(every, None), P(every), P(), P())
    out_specs = (P(every, None), P("y", fsdp, None), P("y", fsdp, None))
    return jax.shard_map(per_device, mesh=fine, in_specs=in_specs, out_specs=out_specs, check_vma=False)
```

```python
import jax
import jax.numpy as jnp
from jax import lax
from jax.experimental import pallas as pl
from jax.experimental.pallas import tpu as pltpu
from jax.sharding import Mesh, PartitionSpec as P

RANK = 64
SCALE = 0.5
BF = jnp.bfloat16
F32 = jnp.float32
SLOTS = 4
INFO = 16
MIB = 1 << 20
SWAP = [(0, 1), (1, 0)]


def dot(a, b, dims=((1,), (0,))):
    return lax.dot_general(a, b, (dims, ((), ())), preferred_element_type=F32)


def exchange(a, axis):
    return lax.all_to_all(a, axis, 0, 0, tiled=True)


def call(body, out, grid, in_specs, out_specs, scratch=(), flops=0, data=0, vmem=40):
    return pl.pallas_call(
        body,
        out_shape=out,
        grid=grid,
        in_specs=in_specs,
        out_specs=out_specs,
        scratch_shapes=list(scratch),
        compiler_params=pltpu.CompilerParams(vmem_limit_bytes=vmem * MIB),
        cost_estimate=pl.CostEstimate(flops=flops, bytes_accessed=data, transcendentals=0),
    )


def whole(shape):
    return pl.BlockSpec(shape, lambda *i: (0,) * len(shape))


def terms(tokens, down, low_t, scaled, tasks_col, pick_t, me_c, nx, nz):
    n_tok, width = tokens.shape
    cols = down.shape[1]
    sc = low_t.shape[0]
    kv = scaled.shape[1]
    steps = nx * nz
    blk = width // steps
    d = blk // 2
    half = kv // 2
    u = half // nz
    lanes = nx * d + u

    def body(me, tok, dn, low, sca, task, pick, hidden, theirs, mine, acc):
        i = pl.program_id(0)
        x, z = i // nz, i % nz
        first = me[0] == 0

        @pl.when(i == 0)
        def _():
            acc[...] = jnp.zeros_like(acc)

        t = tok[...]
        acc[...] += dot(t, dn[...])
        r = dot(low[...], t)
        at = pl.ds(pl.multiple_of(x * d, d), d)
        mine[z, :, at] = jnp.where(first, r[:, :d], r[:, d:])
        theirs[z, :, at] = jnp.where(first, r[:, d:], r[:, :d]).astype(BF)

        @pl.when(i == steps - 1)
        def _():
            adapter = lax.broadcasted_iota(jnp.int32, (n_tok, cols), 1) // RANK
            h = jnp.where(task[...] == adapter, acc[...], 0.0).astype(BF)
            hidden[...] = h
            h_t = dot(pick[...], h, ((1,), (1,))).astype(BF)
            g = dot(h_t, sca[...])
            for k in range(nz):
                a, b = g[:, k * u : (k + 1) * u], g[:, half + k * u : half + (k + 1) * u]
                mine[k, :, nx * d :] = jnp.where(first, a, b)
                theirs[k, :, nx * d :] = jnp.where(first, b, a).astype(BF)

    return call(
        body,
        (
            jax.ShapeDtypeStruct((n_tok, cols), BF),
            jax.ShapeDtypeStruct((nz, sc, lanes), BF),
            jax.ShapeDtypeStruct((nz, sc, lanes), F32),
        ),
        (steps,),
        [
            pl.BlockSpec(memory_space=pltpu.SMEM),
            pl.BlockSpec((n_tok, blk), lambda i: (0, i)),
            pl.BlockSpec((blk, cols), lambda i: (i, 0)),
            whole((sc, n_tok)),
            whole((n_tok, kv)),
            whole((n_tok, 1)),
            whole((sc, cols)),
        ],
        (whole((n_tok, cols)), whole((nz, sc, lanes)), whole((nz, sc, lanes))),
        [pltpu.VMEM((n_tok, cols), F32)],
        flops=2 * n_tok * width * (cols + sc),
        data=28 * MIB,
        vmem=48,
    )(me_c, tokens, down, low_t, scaled, tasks_col, pick_t)


def pack(mine, theirs, note):
    n, sc, lanes = mine.shape

    def body(a, b, c, out):
        out[0, :sc] = (a[0] + b[0].astype(F32)).astype(BF)
        out[0, sc:] = c[...]

    block = pl.BlockSpec((1, sc, lanes), lambda i: (i, 0, 0))
    return call(
        body,
        jax.ShapeDtypeStruct((n, sc + INFO, lanes), BF),
        (n,),
        [block, block, whole((INFO, lanes))],
        pl.BlockSpec((1, sc + INFO, lanes), lambda i: (i, 0, 0)),
        data=10 * MIB,
    )(mine, theirs, note)


def spread(got, owned_col, ny):
    n, rows, lanes = got.shape
    sc = rows - INFO
    cols = owned_col.shape[0]
    own = cols // ny

    def body(g, ow, out):
        total = jnp.zeros((own, lanes), F32)
        flag = jnp.zeros((1, lanes), BF)
        same = (
            lax.broadcasted_iota(jnp.int32, (own, sc), 0) % RANK
            == lax.broadcasted_iota(jnp.int32, (own, sc), 1) % RANK
        )
        for p in range(n):
            note = g[p, sc:, :]
            sent = note[0:1, :sc].astype(F32)
            place = jnp.where(same & (ow[...] == sent), 1.0, 0.0).astype(BF)
            total += dot(place, g[p, :sc, :])
            flag = jnp.maximum(flag, note[1:2, :])
        out[0, :own] = total.astype(BF)
        out[0, own:] = jnp.broadcast_to(flag, (INFO, lanes))

    return call(
        body,
        jax.ShapeDtypeStruct((ny, own + INFO, lanes), BF),
        (ny,),
        [whole((n, rows, lanes)), pl.BlockSpec((own, 1), lambda i: (i, 0))],
        pl.BlockSpec((1, own + INFO, lanes), lambda i: (i, 0, 0)),
        flops=2 * cols * n * sc * lanes,
        data=5 * MIB,
    )(got, owned_col)


def turn(got, nx, d):
    n, rows, lanes = got.shape
    own = rows - INFO
    v = (lanes - nx * d) // nx

    def body(g, out):
        total = g[0, :own].astype(F32)
        flag = g[0, own : own + INFO, :own]
        for p in range(1, n):
            total += g[p, :own].astype(F32)
            flag = jnp.maximum(flag, g[p, own : own + INFO, :own])
        t = total.T.astype(BF)
        for x in range(nx):
            out[x, :d] = t[x * d : (x + 1) * d]
            out[x, d : d + v] = t[nx * d + x * v : nx * d + (x + 1) * v]
            out[x, d + v :] = flag

    return call(
        body,
        jax.ShapeDtypeStruct((nx, d + v + INFO, own), BF),
        (1,),
        [whole(got.shape)],
        whole((nx, d + v + INFO, own)),
        data=2 * MIB,
    )(got)


def finish(got, d):
    n, rows, own = got.shape
    v = rows - INFO - d

    def body(g, down, up, flag):
        total = g[0].astype(F32)
        most = g[0, d + v :].astype(F32)
        for p in range(1, n):
            total += g[p].astype(F32)
            most = jnp.maximum(most, g[p, d + v :].astype(F32))
        down[...] = total[:d]
        up[...] = total[d : d + v]
        flag[...] = most

    shapes = (d, own), (v, own), (INFO, own)
    return call(
        body,
        tuple(jax.ShapeDtypeStruct(s, F32) for s in shapes),
        (1,),
        [whole(got.shape)],
        tuple(whole(s) for s in shapes),
        data=MIB // 2,
    )(got)


def project(tokens, weight, hidden, up):
    n_tok, width = tokens.shape
    kv, cols = up.shape
    blk = 512
    steps = width // blk

    def body(t, w, h, u, out, acc):
        i = pl.program_id(0)

        @pl.when(i == 0)
        def _():
            acc[...] = SCALE * dot(h[...], u[...], ((1,), (1,)))

        acc[...] += dot(t[...], w[...])

        @pl.when(i == steps - 1)
        def _():
            out[...] = acc[...].astype(BF)

    return call(
        body,
        jax.ShapeDtypeStruct((n_tok, kv), BF),
        (steps,),
        [
            pl.BlockSpec((n_tok, blk), lambda i: (0, i)),
            pl.BlockSpec((blk, kv), lambda i: (i, 0)),
            whole((n_tok, cols)),
            whole((kv, cols)),
        ],
        whole((n_tok, kv)),
        [pltpu.VMEM((n_tok, kv), F32)],
        flops=2 * n_tok * kv * (width + cols),
        data=26 * MIB,
    )(tokens, weight, hidden, up)


def per_device(tokens, weight, down, up, cotangent, tasks, owned, counts):
    n_tok, width = tokens.shape
    kv = weight.shape[1]
    adapters = owned.shape[0]
    cols = adapters * RANK
    ny, nx, nz = lax.axis_size("y"), lax.axis_size("x"), lax.axis_size("z")
    me_c = lax.axis_index("c")
    d_rows, v_rows = width // (nx * nz * 2), kv // (nx * nz * 2)
    sc = SLOTS * RANK
    lanes = nx * (d_rows + v_rows)

    full_weight = lax.all_gather(weight, ("x", "z", "c"), axis=0, tiled=True)

    ids = jnp.arange(adapters, dtype=jnp.int32)
    partner_tasks = lax.ppermute(tasks, "c", SWAP)
    hit = tasks[:, None] == ids[None, :]
    present = jnp.any(hit | (partner_tasks[:, None] == ids[None, :]), axis=0)
    rank_of = jnp.sum((ids[None, :] < ids[:, None]) & present[None, :], axis=1)
    col_slot = jnp.arange(sc, dtype=jnp.int32) // RANK
    col_rank = jnp.arange(sc, dtype=jnp.int32) % RANK
    chosen = present[None, :] & (rank_of[None, :] == col_slot[:, None])
    col_task = jnp.sum(jnp.where(chosen, ids[None, :] + 1, 0), axis=1) - 1
    overflow = (jnp.sum(present.astype(jnp.int32)) > SLOTS).astype(F32)

    row = jnp.arange(cols, dtype=jnp.int32)
    pick_t = ((row // RANK)[None, :] == col_task[:, None]) & ((row % RANK)[None, :] == col_rank[:, None])
    pick_t = pick_t.astype(BF)
    mask_slot_t = (tasks[None, :] == col_task[:, None]).astype(F32)

    token_count = jnp.sum(jnp.where(hit, counts.astype(F32)[None, :], 0.0), axis=1)
    scaled = (cotangent.astype(F32) * (SCALE / token_count)[:, None]).astype(BF)
    v_in = jnp.arange(kv, dtype=jnp.int32)
    v_from = (
        (v_in // v_rows % nx) * (nz * 2 * v_rows)
        + (v_in // (v_rows * nx) % nz) * (2 * v_rows)
        + v_in // (v_rows * nx * nz) * v_rows
        + v_in % v_rows
    )
    scaled_by_core = dot(scaled, (v_in[:, None] == v_from[None, :]).astype(BF)).astype(BF)

    up_slot_t = dot(pick_t, up, ((1,), (1,))).astype(BF)
    low_t = (dot(up_slot_t, scaled, ((1,), (1,))) * mask_slot_t).astype(BF)

    hidden, theirs, mine = terms(
        tokens, down, low_t, scaled_by_core, tasks[:, None], pick_t, me_c.astype(jnp.int32)[None], nx, nz
    )

    note_row = lax.broadcasted_iota(jnp.int32, (INFO, lanes), 0)
    note = jnp.where(note_row == 0, jnp.pad(col_task.astype(F32), (0, lanes - sc))[None, :], overflow)
    chip = pack(mine, lax.ppermute(theirs, "c", SWAP), note.astype(BF))

    owned_col = jnp.repeat(owned.astype(F32), RANK)[:, None]
    by_owner = spread(exchange(chip, "z"), owned_col, ny)
    by_x = turn(exchange(by_owner, "y"), nx, d_rows)
    grad_down, grad_up, flags = finish(exchange(by_x, "x"), d_rows)

    keys = project(tokens, full_weight, hidden, up)

    flag, keys = lax.optimization_barrier((flags[0, 0], keys))

    def rest(grads):
        own = cols // ny
        left = jnp.all(tasks[:, None] != col_task[None, :], axis=1)[:, None]
        mask = (tasks[:, None] == (row // RANK)[None, :]) & left
        order = ((row // RANK)[:, None] == owned[row // RANK][None, :]) & (
            (row % RANK)[:, None] == (row % RANK)[None, :]
        )
        order = order.astype(BF)
        low_left = jnp.where(mask, dot(scaled, up), 0.0).astype(BF)
        low_left = dot(low_left, order).astype(BF)
        hid_left = dot(jnp.where(left, hidden, 0.0).astype(BF), order).astype(BF)

        def summed(a, b):
            t = lax.dot_general(
                a, b.reshape(n_tok, ny, own), (((0,), (0,)), ((), ())), preferred_element_type=F32
            )
            t = jnp.transpose(t, (1, 0, 2)).reshape(-1, own)
            for axis in ("y", "x", "z", "c"):
                t = lax.psum_scatter(t, axis, scatter_dimension=0, tiled=True)
            return t

        return grads[0] + summed(tokens, low_left), grads[1] + summed(scaled, hid_left)

    grad_down, grad_up = lax.cond(flag > 0.5, rest, lambda g: g, (grad_down, grad_up))
    return keys, grad_down[None], grad_up[None]


def solution(mesh):
    sizes = dict(mesh.shape)
    ny = sizes["grp"]
    nx = nz = int((sizes["fsdp"] // 2) ** 0.5)
    fine = Mesh(mesh.devices.reshape(ny, nx, nz, 2), ("y", "x", "z", "c"))
    fsdp = ("x", "z", "c")
    every = ("y", "x", "z", "c")
    in_specs = (P(every, None), P(fsdp, None), P(), P(), P(every, None), P(every), P(), P())
    out_specs = (P(every, None), P("y", fsdp, None), P("y", fsdp, None))
    return jax.shard_map(per_device, mesh=fine, in_specs=in_specs, out_specs=out_specs, check_vma=False)
```

```python
import jax
import jax.numpy as jnp
from jax import lax
from jax.experimental import pallas as pl
from jax.experimental.pallas import tpu as pltpu
from jax.sharding import Mesh, PartitionSpec as P

RANK = 64
SCALE = 0.5
BF = jnp.bfloat16
F32 = jnp.float32
SLOTS = 2
INFO = 16
MIB = 1 << 20
SWAP = [(0, 1), (1, 0)]


def dot(a, b, dims=((1,), (0,))):
    return lax.dot_general(a, b, (dims, ((), ())), preferred_element_type=F32)


def exchange(a, axis):
    return lax.all_to_all(a, axis, 0, 0, tiled=True)


def call(body, out, grid, in_specs, out_specs, scratch=(), flops=0, data=0, vmem=40):
    return pl.pallas_call(
        body,
        out_shape=out,
        grid=grid,
        in_specs=in_specs,
        out_specs=out_specs,
        scratch_shapes=list(scratch),
        compiler_params=pltpu.CompilerParams(vmem_limit_bytes=vmem * MIB),
        cost_estimate=pl.CostEstimate(flops=flops, bytes_accessed=data, transcendentals=0),
    )


def whole(shape):
    return pl.BlockSpec(shape, lambda *i: (0,) * len(shape))


def terms(tokens, down, low_t, scaled, tasks_col, pick_t, me_c, nx, nz):
    n_tok, width = tokens.shape
    cols = down.shape[1]
    sc = low_t.shape[0]
    kv = scaled.shape[1]
    per = 2
    steps = nx * nz // per
    blk = width // steps
    d = width // (nx * nz * 2)
    half = kv // 2
    u = half // nz
    lanes = nx * d + u

    def body(me, tok, dn, low, sca, task, pick, hidden, theirs, mine, acc):
        i = pl.program_id(0)
        first = me[0] == 0
        t = tok[...]
        part = dot(t, dn[...])

        @pl.when(i == 0)
        def _():
            acc[...] = part

        @pl.when(i > 0)
        def _():
            acc[...] += part

        r = dot(low[...], t)
        for k in range(per):
            x, z = (i * per + k) // nz, (i * per + k) % nz
            at = pl.ds(pl.multiple_of(x * d, d), d)
            a, b = r[:, 2 * k * d : (2 * k + 1) * d], r[:, (2 * k + 1) * d : (2 * k + 2) * d]
            mine[z, :, at] = jnp.where(first, a, b)
            theirs[z, :, at] = jnp.where(first, b, a).astype(BF)

        @pl.when(i == steps - 1)
        def _():
            adapter = lax.broadcasted_iota(jnp.int32, (n_tok, cols), 1) // RANK
            h = jnp.where(task[...] == adapter, acc[...], 0.0).astype(BF)
            hidden[...] = h
            h_t = dot(pick[...], h, ((1,), (1,))).astype(BF)
            g = dot(h_t, sca[...])
            for k in range(nz):
                a, b = g[:, k * u : (k + 1) * u], g[:, half + k * u : half + (k + 1) * u]
                mine[k, :, nx * d :] = jnp.where(first, a, b)
                theirs[k, :, nx * d :] = jnp.where(first, b, a).astype(BF)

    return call(
        body,
        (
            jax.ShapeDtypeStruct((n_tok, cols), BF),
            jax.ShapeDtypeStruct((nz, sc, lanes), BF),
            jax.ShapeDtypeStruct((nz, sc, lanes), F32),
        ),
        (steps,),
        [
            pl.BlockSpec(memory_space=pltpu.SMEM),
            pl.BlockSpec((n_tok, blk), lambda i: (0, i)),
            pl.BlockSpec((blk, cols), lambda i: (i, 0)),
            whole((sc, n_tok)),
            whole((n_tok, kv)),
            whole((n_tok, 1)),
            whole((sc, cols)),
        ],
        (whole((n_tok, cols)), whole((nz, sc, lanes)), whole((nz, sc, lanes))),
        [pltpu.VMEM((n_tok, cols), F32)],
        flops=2 * n_tok * width * (cols + sc),
        data=28 * MIB,
        vmem=48,
    )(me_c, tokens, down, low_t, scaled, tasks_col, pick_t)


def pack(mine, theirs, note):
    n, sc, lanes = mine.shape

    def body(a, b, c, out):
        out[0, :sc] = (a[0] + b[0].astype(F32)).astype(BF)
        out[0, sc:] = c[...]

    block = pl.BlockSpec((1, sc, lanes), lambda i: (i, 0, 0))
    return call(
        body,
        jax.ShapeDtypeStruct((n, sc + INFO, lanes), BF),
        (n,),
        [block, block, whole((INFO, lanes))],
        pl.BlockSpec((1, sc + INFO, lanes), lambda i: (i, 0, 0)),
        data=10 * MIB,
    )(mine, theirs, note)


def spread(got, owned_col, ny):
    n, rows, lanes = got.shape
    sc = rows - INFO
    cols = owned_col.shape[0]
    own = cols // ny

    def body(g, ow, out):
        total = jnp.zeros((own, lanes), F32)
        flag = jnp.zeros((1, lanes), BF)
        same = (
            lax.broadcasted_iota(jnp.int32, (own, sc), 0) % RANK
            == lax.broadcasted_iota(jnp.int32, (own, sc), 1) % RANK
        )
        for p in range(n):
            note = g[p, sc:, :]
            sent = note[0:1, :sc].astype(F32)
            place = jnp.where(same & (ow[...] == sent), 1.0, 0.0).astype(BF)
            total += dot(place, g[p, :sc, :])
            flag = jnp.maximum(flag, note[1:2, :])
        out[0, :own] = total.astype(BF)
        out[0, own:] = jnp.broadcast_to(flag, (INFO, lanes))

    return call(
        body,
        jax.ShapeDtypeStruct((ny, own + INFO, lanes), BF),
        (ny,),
        [whole((n, rows, lanes)), pl.BlockSpec((own, 1), lambda i: (i, 0))],
        pl.BlockSpec((1, own + INFO, lanes), lambda i: (i, 0, 0)),
        flops=2 * cols * n * sc * lanes,
        data=5 * MIB,
    )(got, owned_col)


def turn(got, nx, d):
    n, rows, lanes = got.shape
    own = rows - INFO
    v = (lanes - nx * d) // nx

    def body(g, out):
        total = g[0, :own].astype(F32)
        flag = g[0, own : own + INFO, :own]
        for p in range(1, n):
            total += g[p, :own].astype(F32)
            flag = jnp.maximum(flag, g[p, own : own + INFO, :own])
        t = total.T.astype(BF)
        for x in range(nx):
            out[x, :d] = t[x * d : (x + 1) * d]
            out[x, d : d + v] = t[nx * d + x * v : nx * d + (x + 1) * v]
            out[x, d + v :] = flag

    return call(
        body,
        jax.ShapeDtypeStruct((nx, d + v + INFO, own), BF),
        (1,),
        [whole(got.shape)],
        whole((nx, d + v + INFO, own)),
        data=2 * MIB,
    )(got)


def finish(got, d):
    n, rows, own = got.shape
    v = rows - INFO - d

    def body(g, down, up, flag):
        total = g[0].astype(F32)
        most = g[0, d + v :].astype(F32)
        for p in range(1, n):
            total += g[p].astype(F32)
            most = jnp.maximum(most, g[p, d + v :].astype(F32))
        down[...] = total[:d]
        up[...] = total[d : d + v]
        flag[...] = most

    shapes = (d, own), (v, own), (INFO, own)
    return call(
        body,
        tuple(jax.ShapeDtypeStruct(s, F32) for s in shapes),
        (1,),
        [whole(got.shape)],
        tuple(whole(s) for s in shapes),
        data=MIB // 2,
    )(got)


def shifted(a, axis, step):
    n = lax.axis_size(axis)
    return lax.ppermute(a, axis, [(i, (i + step) % n) for i in range(n)])


def add_blocks(own, other, groups, where_from, before=None, lora=None, final=False):
    n_tok = own.shape[0]
    rows = sum(w.shape[0] for w in groups[0])
    n = groups[0][0].shape[1]
    steps = len(groups)
    per = where_from.shape[0] // steps
    blk = rows // per
    flat = [w for group in groups for w in group]
    extra = [] if before is None else [before]
    if lora is not None:
        extra += list(lora)

    def body(at, *refs):
        tok_a, tok_b = refs[:per], refs[per : 2 * per]
        ws = refs[2 * per : 2 * per + len(flat)]
        more = refs[2 * per + len(flat) : 2 * per + len(flat) + len(extra)]
        out = refs[2 * per + len(flat) + len(extra)]
        acc = refs[-1]
        i = pl.program_id(0)

        @pl.when(i == 0)
        def _():
            if before is not None:
                acc[...] = more[0][...]
            else:
                acc[...] = jnp.zeros_like(acc)
            if lora is not None:
                h_a, h_b, u = more[-3:]
                acc[:n_tok] += SCALE * dot(h_a[...], u[...], ((1,), (1,)))
                acc[n_tok:] += SCALE * dot(h_b[...], u[...], ((1,), (1,)))

        left = 0
        for p in range(steps):
            mine = ws[left : left + len(groups[p])]
            left += len(groups[p])

            @pl.when(i == p)
            def _(mine=mine):
                parts = [w[...] for w in mine]
                w = parts[0] if len(parts) == 1 else jnp.concatenate(parts, axis=0)
                acc[:n_tok] += dot(jnp.concatenate([t[...] for t in tok_a], axis=1), w)
                acc[n_tok:] += dot(jnp.concatenate([t[...] for t in tok_b], axis=1), w)

        if final:

            @pl.when(i == steps - 1)
            def _():
                out[...] = acc[...].astype(BF)

    tok_specs = [pl.BlockSpec((n_tok, blk), lambda i, s, k=k: (0, s[i * per + k])) for k in range(per)]
    shape = (2 * n_tok, n)
    return pl.pallas_call(
        body,
        out_shape=jax.ShapeDtypeStruct(shape, BF if final else F32),
        grid_spec=pltpu.PrefetchScalarGridSpec(
            num_scalar_prefetch=1,
            grid=(steps,),
            in_specs=tok_specs * 2 + [whole(w.shape) for w in flat] + [whole(e.shape) for e in extra],
            out_specs=whole(shape),
            scratch_shapes=[pltpu.VMEM(shape, F32)] if final else [],
        ),
        compiler_params=pltpu.CompilerParams(vmem_limit_bytes=40 * MIB),
        cost_estimate=pl.CostEstimate(
            flops=4 * n_tok * rows * n * steps, bytes_accessed=8 * n_tok * rows * steps, transcendentals=0
        ),
    )(where_from, *([own] * per), *([other] * per), *flat, *extra)


def per_device(tokens, weight, down, up, cotangent, tasks, owned, counts):
    n_tok, width = tokens.shape
    kv = weight.shape[1]
    adapters = owned.shape[0]
    cols = adapters * RANK
    ny, nx, nz = lax.axis_size("y"), lax.axis_size("x"), lax.axis_size("z")
    me_c = lax.axis_index("c")
    d_rows, v_rows = width // (nx * nz * 2), kv // (nx * nz * 2)
    me_x, me_z = lax.axis_index("x"), lax.axis_index("z")
    sc = SLOTS * RANK
    lanes = nx * (d_rows + v_rows)
    half = kv // 2

    def columns(a, core):
        return lax.dynamic_slice_in_dim(a, core * half, half, 1)

    block_a = columns(weight, me_c)
    block_b = lax.ppermute(columns(weight, 1 - me_c), "c", SWAP)
    near_a = jnp.concatenate([block_a] + [shifted(block_a, "x", k) for k in range(1, nx)])
    near_b = jnp.concatenate([block_b] + [shifted(block_b, "z", k) for k in range(1, nz)])
    cut_a, cut_b = near_a.shape[0] // 2, near_b.shape[0] // 2
    a_down, a_up = shifted(near_a, "z", 1), shifted(near_a, "z", nz - 1)
    b_down, b_up = shifted(near_b, "x", 1), shifted(near_b, "x", nx - 1)
    a_far = [shifted(a_down[:cut_a], "z", 1), shifted(a_up[cut_a:], "z", nz - 1)]
    b_far = [shifted(b_down[:cut_b], "x", 1), shifted(b_up[cut_b:], "x", nx - 1)]

    def blocks_a(step):
        z = (me_z + step) % nz
        return [(((me_x - k) % nx) * nz + z) * 2 + me_c for k in range(nx)]

    def blocks_b(step):
        x = (me_x + step) % nx
        return [(x * nz + (me_z - k) % nz) * 2 + 1 - me_c for k in range(nz)]

    def at(*lists):
        return jnp.stack([i for one in lists for i in one]).astype(jnp.int32)

    ids = jnp.arange(adapters, dtype=jnp.int32)
    partner_tasks = lax.ppermute(tasks, "c", SWAP)
    hit = tasks[:, None] == ids[None, :]
    present = jnp.any(hit | (partner_tasks[:, None] == ids[None, :]), axis=0)
    rank_of = jnp.sum((ids[None, :] < ids[:, None]) & present[None, :], axis=1)
    col_slot = jnp.arange(sc, dtype=jnp.int32) // RANK
    col_rank = jnp.arange(sc, dtype=jnp.int32) % RANK
    row = jnp.arange(cols, dtype=jnp.int32)

    token_count = jnp.sum(jnp.where(hit, counts.astype(F32)[None, :], 0.0), axis=1)
    scaled = (cotangent.astype(F32) * (SCALE / token_count)[:, None]).astype(BF)
    v_in = jnp.arange(kv, dtype=jnp.int32)
    v_from = (
        (v_in // v_rows % nx) * (nz * 2 * v_rows)
        + (v_in // (v_rows * nx) % nz) * (2 * v_rows)
        + v_in // (v_rows * nx * nz) * v_rows
        + v_in % v_rows
    )
    scaled_by_core = dot(scaled, (v_in[:, None] == v_from[None, :]).astype(BF)).astype(BF)

    owned_col = jnp.repeat(owned.astype(F32), RANK)[:, None]

    def round_of(first, after):
        chosen = present[None, :] & (rank_of[None, :] == first + col_slot[:, None])
        col_task = jnp.sum(jnp.where(chosen, ids[None, :] + 1, 0), axis=1) - 1
        more = (jnp.sum(present.astype(jnp.int32)) > first + SLOTS).astype(F32)
        pick_t = ((row // RANK)[None, :] == col_task[:, None]) & ((row % RANK)[None, :] == col_rank[:, None])
        pick_t = pick_t.astype(BF)
        mask_slot_t = (tasks[None, :] == col_task[:, None]).astype(F32)
        up_slot_t = dot(pick_t, up, ((1,), (1,))).astype(BF)
        low_t = (dot(up_slot_t, scaled, ((1,), (1,))) * mask_slot_t).astype(BF)
        low_t, _ = lax.optimization_barrier((low_t, after))
        hidden, theirs, mine = terms(
            tokens, down, low_t, scaled_by_core, tasks[:, None], pick_t, me_c.astype(jnp.int32)[None], nx, nz
        )
        note_row = lax.broadcasted_iota(jnp.int32, (INFO, lanes), 0)
        note = jnp.where(note_row == 0, jnp.pad(col_task.astype(F32), (0, lanes - sc))[None, :], more)
        got = lax.ppermute(theirs, "c", SWAP)
        chip = pack(mine, got, note.astype(BF))
        by_owner = spread(exchange(chip, "z"), owned_col, ny)
        by_x = turn(exchange(by_owner, "y"), nx, d_rows)
        grad_down, grad_up, flags = finish(exchange(by_x, "x"), d_rows)
        return hidden, got, grad_down, grad_up, flags[0, 0]

    hidden, got, grad_down, grad_up, flag = round_of(jnp.int32(0), (near_a, near_b))

    sent_tokens, sent_hidden, _ = lax.optimization_barrier((tokens, hidden, got))
    other = lax.ppermute(sent_tokens, "c", SWAP)
    other_hidden = lax.ppermute(sent_hidden, "c", SWAP)
    acc = add_blocks(tokens, other, [[near_a], [near_b]], at(blocks_a(0), blocks_b(0)))
    acc = add_blocks(
        tokens,
        other,
        [[a_down], [a_up], [b_down], [b_up]],
        at(blocks_a(-1), blocks_a(1), blocks_b(-1), blocks_b(1)),
        before=acc,
        lora=(hidden, other_hidden, lax.dynamic_slice_in_dim(up, me_c * half, half, 0)),
    )
    tile = add_blocks(tokens, other, [a_far, b_far], at(blocks_a(2), blocks_b(2)), before=acc, final=True)
    back = lax.ppermute(tile[n_tok:], "c", SWAP)
    low_half = jnp.where(me_c == 0, tile[:n_tok], back)
    high_half = jnp.where(me_c == 0, back, tile[:n_tok])
    keys = jnp.concatenate([low_half, high_half], axis=1)

    flag, keys = lax.optimization_barrier((flag, keys))

    def again(state):
        first, down_sum, up_sum, _ = state
        _, _, down_more, up_more, flag = round_of(first, ())
        return first + SLOTS, down_sum + down_more, up_sum + up_more, flag

    _, grad_down, grad_up, _ = lax.while_loop(
        lambda state: state[3] > 0.5, again, (jnp.int32(SLOTS), grad_down, grad_up, flag)
    )
    return keys, grad_down[None], grad_up[None]


def solution(mesh):
    sizes = dict(mesh.shape)
    ny = sizes["grp"]
    nx = nz = int((sizes["fsdp"] // 2) ** 0.5)
    fine = Mesh(mesh.devices.reshape(ny, nx, nz, 2), ("y", "x", "z", "c"))
    fsdp = ("x", "z", "c")
    every = ("y", "x", "z", "c")
    in_specs = (P(every, None), P(fsdp, None), P(), P(), P(every, None), P(every), P(), P())
    out_specs = (P(every, None), P("y", fsdp, None), P("y", fsdp, None))
    return jax.shard_map(per_device, mesh=fine, in_specs=in_specs, out_specs=out_specs, check_vma=False)
```

```python
import jax
import jax.numpy as jnp
from jax import lax
from jax.experimental import pallas as pl
from jax.experimental.pallas import tpu as pltpu
from jax.sharding import Mesh, PartitionSpec as P

RANK = 64
SCALE = 0.5
BF = jnp.bfloat16
F32 = jnp.float32
SLOTS = 2
INFO = 16
MIB = 1 << 20
SWAP = [(0, 1), (1, 0)]


def dot(a, b, dims=((1,), (0,))):
    return lax.dot_general(a, b, (dims, ((), ())), preferred_element_type=F32)


def exchange(a, axis):
    return lax.all_to_all(a, axis, 0, 0, tiled=True)


def call(body, out, grid, in_specs, out_specs, scratch=(), flops=0, data=0, vmem=40):
    return pl.pallas_call(
        body,
        out_shape=out,
        grid=grid,
        in_specs=in_specs,
        out_specs=out_specs,
        scratch_shapes=list(scratch),
        compiler_params=pltpu.CompilerParams(vmem_limit_bytes=vmem * MIB),
        cost_estimate=pl.CostEstimate(flops=flops, bytes_accessed=data, transcendentals=0),
    )


def whole(shape):
    return pl.BlockSpec(shape, lambda *i: (0,) * len(shape))


def terms(tokens, down, low_t, scaled, tasks_col, pick_t, me_c, nx, nz):
    n_tok, width = tokens.shape
    cols = down.shape[1]
    sc = low_t.shape[0]
    kv = scaled.shape[1]
    per = 4
    steps = nx * nz // per
    blk = width // steps
    d = width // (nx * nz * 2)
    half = kv // 2
    u = half // nz
    lanes = nx * d + u

    def body(me, tok, dn, low, sca, task, pick, hidden, theirs, mine, acc):
        i = pl.program_id(0)
        first = me[0] == 0
        t = tok[...]
        part = dot(t, dn[...])

        @pl.when(i == 0)
        def _():
            acc[...] = part

        @pl.when(i > 0)
        def _():
            acc[...] += part

        r = dot(low[...], t)
        for k in range(per):
            x, z = (i * per + k) // nz, (i * per + k) % nz
            at = pl.ds(pl.multiple_of(x * d, d), d)
            a, b = r[:, 2 * k * d : (2 * k + 1) * d], r[:, (2 * k + 1) * d : (2 * k + 2) * d]
            mine[z, :, at] = jnp.where(first, a, b).astype(BF)
            theirs[z, :, at] = jnp.where(first, b, a).astype(BF)

        @pl.when(i == steps - 1)
        def _():
            adapter = lax.broadcasted_iota(jnp.int32, (n_tok, cols), 1) // RANK
            h = jnp.where(task[...] == adapter, acc[...], 0.0).astype(BF)
            hidden[...] = h
            h_t = dot(pick[...], h, ((1,), (1,))).astype(BF)
            g = dot(h_t, sca[...])
            for k in range(nz):
                a, b = g[:, k * u : (k + 1) * u], g[:, half + k * u : half + (k + 1) * u]
                mine[k, :, nx * d :] = jnp.where(first, a, b).astype(BF)
                theirs[k, :, nx * d :] = jnp.where(first, b, a).astype(BF)

    return call(
        body,
        (
            jax.ShapeDtypeStruct((n_tok, cols), BF),
            jax.ShapeDtypeStruct((nz, sc, lanes), BF),
            jax.ShapeDtypeStruct((nz, sc, lanes), BF),
        ),
        (steps,),
        [
            pl.BlockSpec(memory_space=pltpu.SMEM),
            pl.BlockSpec((n_tok, blk), lambda i: (0, i)),
            pl.BlockSpec((blk, cols), lambda i: (i, 0)),
            whole((sc, n_tok)),
            whole((n_tok, kv)),
            whole((n_tok, 1)),
            whole((sc, cols)),
        ],
        (whole((n_tok, cols)), whole((nz, sc, lanes)), whole((nz, sc, lanes))),
        [pltpu.VMEM((n_tok, cols), F32)],
        flops=2 * n_tok * width * (cols + sc),
        data=28 * MIB,
        vmem=48,
    )(me_c, tokens, down, low_t, scaled, tasks_col, pick_t)


def pack(mine, theirs, note):
    n, sc, lanes = mine.shape

    def body(a, b, c, out):
        out[0, :sc] = (a[0].astype(F32) + b[0].astype(F32)).astype(BF)
        out[0, sc:] = c[...]

    block = pl.BlockSpec((1, sc, lanes), lambda i: (i, 0, 0))
    return call(
        body,
        jax.ShapeDtypeStruct((n, sc + INFO, lanes), BF),
        (n,),
        [block, block, whole((INFO, lanes))],
        pl.BlockSpec((1, sc + INFO, lanes), lambda i: (i, 0, 0)),
        data=10 * MIB,
    )(mine, theirs, note)


def spread(got, owned_col, ny):
    n, rows, lanes = got.shape
    sc = rows - INFO
    cols = owned_col.shape[0]
    own = cols // ny

    def body(g, ow, out):
        total = jnp.zeros((own, lanes), F32)
        flag = jnp.zeros((1, lanes), BF)
        same = (
            lax.broadcasted_iota(jnp.int32, (own, sc), 0) % RANK
            == lax.broadcasted_iota(jnp.int32, (own, sc), 1) % RANK
        )
        for p in range(n):
            note = g[p, sc:, :]
            sent = note[0:1, :sc].astype(F32)
            place = jnp.where(same & (ow[...] == sent), 1.0, 0.0).astype(BF)
            total += dot(place, g[p, :sc, :])
            flag = jnp.maximum(flag, note[1:2, :])
        out[0, :own] = total.astype(BF)
        out[0, own:] = jnp.broadcast_to(flag, (INFO, lanes))

    return call(
        body,
        jax.ShapeDtypeStruct((ny, own + INFO, lanes), BF),
        (ny,),
        [whole((n, rows, lanes)), pl.BlockSpec((own, 1), lambda i: (i, 0))],
        pl.BlockSpec((1, own + INFO, lanes), lambda i: (i, 0, 0)),
        flops=2 * cols * n * sc * lanes,
        data=5 * MIB,
    )(got, owned_col)


def turn(got, nx, d):
    n, rows, lanes = got.shape
    own = rows - INFO
    v = (lanes - nx * d) // nx

    def body(g, out):
        total = g[0, :own].astype(F32)
        flag = g[0, own : own + INFO, :own]
        for p in range(1, n):
            total += g[p, :own].astype(F32)
            flag = jnp.maximum(flag, g[p, own : own + INFO, :own])
        t = total.T.astype(BF)
        for x in range(nx):
            out[x, :d] = t[x * d : (x + 1) * d]
            out[x, d : d + v] = t[nx * d + x * v : nx * d + (x + 1) * v]
            out[x, d + v :] = flag

    return call(
        body,
        jax.ShapeDtypeStruct((nx, d + v + INFO, own), BF),
        (1,),
        [whole(got.shape)],
        whole((nx, d + v + INFO, own)),
        data=2 * MIB,
    )(got)


def finish(got, d):
    n, rows, own = got.shape
    v = rows - INFO - d

    def body(g, down, up, flag):
        total = g[0].astype(F32)
        most = g[0, d + v :].astype(F32)
        for p in range(1, n):
            total += g[p].astype(F32)
            most = jnp.maximum(most, g[p, d + v :].astype(F32))
        down[...] = total[:d]
        up[...] = total[d : d + v]
        flag[...] = most

    shapes = (d, own), (v, own), (INFO, own)
    return call(
        body,
        tuple(jax.ShapeDtypeStruct(s, F32) for s in shapes),
        (1,),
        [whole(got.shape)],
        tuple(whole(s) for s in shapes),
        data=MIB // 2,
    )(got)


def shifted(a, axis, step):
    n = lax.axis_size(axis)
    return lax.ppermute(a, axis, [(i, (i + step) % n) for i in range(n)])


def add_blocks(own, other, groups, where_from, before=None, lora=None, final=False):
    n_tok = own.shape[0]
    rows = sum(w.shape[0] for w in groups[0])
    n = groups[0][0].shape[1]
    steps = len(groups)
    per = where_from.shape[0] // steps
    blk = rows // per
    flat = [w for group in groups for w in group]
    extra = [] if before is None else [before]
    if lora is not None:
        extra += list(lora)

    def body(at, *refs):
        tok_a, tok_b = refs[:per], refs[per : 2 * per]
        ws = refs[2 * per : 2 * per + len(flat)]
        more = refs[2 * per + len(flat) : 2 * per + len(flat) + len(extra)]
        out = refs[2 * per + len(flat) + len(extra)]
        acc = refs[-1]
        i = pl.program_id(0)

        @pl.when(i == 0)
        def _():
            if before is not None:
                acc[...] = more[0][...]
            else:
                acc[...] = jnp.zeros_like(acc)
            if lora is not None:
                h_a, h_b, u = more[-3:]
                acc[:n_tok] += SCALE * dot(h_a[...], u[...], ((1,), (1,)))
                acc[n_tok:] += SCALE * dot(h_b[...], u[...], ((1,), (1,)))

        left = 0
        for p in range(steps):
            mine = ws[left : left + len(groups[p])]
            left += len(groups[p])

            @pl.when(i == p)
            def _(mine=mine):
                parts = [w[...] for w in mine]
                w = parts[0] if len(parts) == 1 else jnp.concatenate(parts, axis=0)
                acc[:n_tok] += dot(jnp.concatenate([t[...] for t in tok_a], axis=1), w)
                acc[n_tok:] += dot(jnp.concatenate([t[...] for t in tok_b], axis=1), w)

        if final:

            @pl.when(i == steps - 1)
            def _():
                out[...] = acc[...].astype(BF)

    tok_specs = [pl.BlockSpec((n_tok, blk), lambda i, s, k=k: (0, s[i * per + k])) for k in range(per)]
    shape = (2 * n_tok, n)
    return pl.pallas_call(
        body,
        out_shape=jax.ShapeDtypeStruct(shape, BF if final else F32),
        grid_spec=pltpu.PrefetchScalarGridSpec(
            num_scalar_prefetch=1,
            grid=(steps,),
            in_specs=tok_specs * 2 + [whole(w.shape) for w in flat] + [whole(e.shape) for e in extra],
            out_specs=whole(shape),
            scratch_shapes=[pltpu.VMEM(shape, F32)] if final else [],
        ),
        compiler_params=pltpu.CompilerParams(vmem_limit_bytes=40 * MIB),
        cost_estimate=pl.CostEstimate(
            flops=4 * n_tok * rows * n * steps, bytes_accessed=8 * n_tok * rows * steps, transcendentals=0
        ),
    )(where_from, *([own] * per), *([other] * per), *flat, *extra)


def per_device(tokens, weight, down, up, cotangent, tasks, owned, counts):
    n_tok, width = tokens.shape
    kv = weight.shape[1]
    adapters = owned.shape[0]
    cols = adapters * RANK
    ny, nx, nz = lax.axis_size("y"), lax.axis_size("x"), lax.axis_size("z")
    me_c = lax.axis_index("c")
    d_rows, v_rows = width // (nx * nz * 2), kv // (nx * nz * 2)
    me_x, me_z = lax.axis_index("x"), lax.axis_index("z")
    sc = SLOTS * RANK
    lanes = nx * (d_rows + v_rows)
    half = kv // 2

    def columns(a, core):
        return lax.dynamic_slice_in_dim(a, core * half, half, 1)

    block_a = columns(weight, me_c)
    block_b = lax.ppermute(columns(weight, 1 - me_c), "c", SWAP)
    partner_tasks = lax.ppermute(tasks, "c", SWAP)
    block_b, partner_tasks, cotangent, counts = lax.optimization_barrier((block_b, partner_tasks, cotangent, counts))
    first_hop = [shifted(block_a, "x", k) for k in range(1, nx)] + [shifted(block_b, "z", k) for k in range(1, nz)]
    def blocks_a(step):
        z = (me_z + step) % nz
        return [(((me_x - k) % nx) * nz + z) * 2 + me_c for k in range(nx)]

    def blocks_b(step):
        x = (me_x + step) % nx
        return [(x * nz + (me_z - k) % nz) * 2 + 1 - me_c for k in range(nz)]

    def at(*lists):
        return jnp.stack([i for one in lists for i in one]).astype(jnp.int32)

    ids = jnp.arange(adapters, dtype=jnp.int32)
    hit = tasks[:, None] == ids[None, :]
    present = jnp.any(hit | (partner_tasks[:, None] == ids[None, :]), axis=0)
    rank_of = jnp.sum((ids[None, :] < ids[:, None]) & present[None, :], axis=1)
    col_slot = jnp.arange(sc, dtype=jnp.int32) // RANK
    col_rank = jnp.arange(sc, dtype=jnp.int32) % RANK
    row = jnp.arange(cols, dtype=jnp.int32)

    token_count = jnp.sum(jnp.where(hit, counts.astype(F32)[None, :], 0.0), axis=1)
    scaled = (cotangent.astype(F32) * (SCALE / token_count)[:, None]).astype(BF)
    v_in = jnp.arange(kv, dtype=jnp.int32)
    v_from = (
        (v_in // v_rows % nx) * (nz * 2 * v_rows)
        + (v_in // (v_rows * nx) % nz) * (2 * v_rows)
        + v_in // (v_rows * nx * nz) * v_rows
        + v_in % v_rows
    )
    scaled_by_core = dot(scaled, (v_in[:, None] == v_from[None, :]).astype(BF)).astype(BF)

    owned_col = jnp.repeat(owned.astype(F32), RANK)[:, None]

    def local_terms(first):
        chosen = present[None, :] & (rank_of[None, :] == first + col_slot[:, None])
        col_task = jnp.sum(jnp.where(chosen, ids[None, :] + 1, 0), axis=1) - 1
        more = (jnp.sum(present.astype(jnp.int32)) > first + SLOTS).astype(F32)
        pick_t = ((row // RANK)[None, :] == col_task[:, None]) & ((row % RANK)[None, :] == col_rank[:, None])
        pick_t = pick_t.astype(BF)
        mask_slot_t = (tasks[None, :] == col_task[:, None]).astype(F32)
        up_slot_t = dot(pick_t, up, ((1,), (1,))).astype(BF)
        low_t = (dot(up_slot_t, scaled, ((1,), (1,))) * mask_slot_t).astype(BF)
        hidden, theirs, mine = terms(
            tokens, down, low_t, scaled_by_core, tasks[:, None], pick_t, me_c.astype(jnp.int32)[None], nx, nz
        )
        note_row = lax.broadcasted_iota(jnp.int32, (INFO, lanes), 0)
        note = jnp.where(note_row == 0, jnp.pad(col_task.astype(F32), (0, lanes - sc))[None, :], more)
        return hidden, theirs, mine, note.astype(BF)

    hidden, theirs, mine, note = local_terms(jnp.int32(0))
    first_hop, theirs = lax.optimization_barrier((first_hop, theirs))
    got = lax.ppermute(theirs, "c", SWAP)
    near_a = jnp.concatenate([block_a] + first_hop[: nx - 1])
    near_b = jnp.concatenate([block_b] + first_hop[nx - 1 :])
    cut_a, cut_b = near_a.shape[0] // 2, near_b.shape[0] // 2
    a_down, a_up = shifted(near_a, "z", 1), shifted(near_a, "z", nz - 1)
    b_down, b_up = shifted(near_b, "x", 1), shifted(near_b, "x", nx - 1)
    a_far = [shifted(a_down[:cut_a], "z", 1), shifted(a_up[cut_a:], "z", nz - 1)]
    b_far = [shifted(b_down[:cut_b], "x", 1), shifted(b_up[cut_b:], "x", nx - 1)]

    from_z = exchange(pack(mine, got, note), "z")

    sent_tokens, sent_hidden, _ = lax.optimization_barrier((tokens, hidden, got))
    other = lax.ppermute(sent_tokens, "c", SWAP)
    other_hidden = lax.ppermute(sent_hidden, "c", SWAP)
    acc = add_blocks(tokens, other, [[near_a], [near_b]], at(blocks_a(0), blocks_b(0)))
    from_z, acc = lax.optimization_barrier((from_z, acc))
    from_y = exchange(spread(from_z, owned_col, ny), "y")
    acc = add_blocks(
        tokens,
        other,
        [[a_down], [a_up], [b_down], [b_up]],
        at(blocks_a(-1), blocks_a(1), blocks_b(-1), blocks_b(1)),
        before=acc,
        lora=(hidden, other_hidden, lax.dynamic_slice_in_dim(up, me_c * half, half, 0)),
    )
    from_y, acc = lax.optimization_barrier((from_y, acc))
    grad_down, grad_up, flags = finish(exchange(turn(from_y, nx, d_rows), "x"), d_rows)
    tile = add_blocks(tokens, other, [a_far, b_far], at(blocks_a(2), blocks_b(2)), before=acc, final=True)
    back = lax.ppermute(tile[n_tok:], "c", SWAP)
    low_half = jnp.where(me_c == 0, tile[:n_tok], back)
    high_half = jnp.where(me_c == 0, back, tile[:n_tok])
    keys = jnp.concatenate([low_half, high_half], axis=1)

    flag, keys = lax.optimization_barrier((flags[0, 0], keys))

    def again(state):
        first, down_sum, up_sum, _ = state
        _, theirs, mine, note = local_terms(first)
        by_owner = spread(exchange(pack(mine, lax.ppermute(theirs, "c", SWAP), note), "z"), owned_col, ny)
        by_x = turn(exchange(by_owner, "y"), nx, d_rows)
        down_more, up_more, flags = finish(exchange(by_x, "x"), d_rows)
        return first + SLOTS, down_sum + down_more, up_sum + up_more, flags[0, 0]

    _, grad_down, grad_up, _ = lax.while_loop(
        lambda state: state[3] > 0.5, again, (jnp.int32(SLOTS), grad_down, grad_up, flag)
    )
    return keys, grad_down[None], grad_up[None]


def solution(mesh):
    sizes = dict(mesh.shape)
    ny = sizes["grp"]
    nx = nz = int((sizes["fsdp"] // 2) ** 0.5)
    fine = Mesh(mesh.devices.reshape(ny, nx, nz, 2), ("y", "x", "z", "c"))
    fsdp = ("x", "z", "c")
    every = ("y", "x", "z", "c")
    in_specs = (P(every, None), P(fsdp, None), P(), P(), P(every, None), P(every), P(), P())
    out_specs = (P(every, None), P("y", fsdp, None), P("y", fsdp, None))
    return jax.shard_map(per_device, mesh=fine, in_specs=in_specs, out_specs=out_specs, check_vma=False)
```

```python
import jax
import jax.numpy as jnp
from jax import lax
from jax.experimental import pallas as pl
from jax.experimental.pallas import tpu as pltpu
from jax.sharding import Mesh, PartitionSpec as P

RANK = 64
SCALE = 0.5
BF = jnp.bfloat16
F32 = jnp.float32
SLOTS = 2
INFO = 16
MIB = 1 << 20
SWAP = [(0, 1), (1, 0)]


def dot(a, b, dims=((1,), (0,))):
    return lax.dot_general(a, b, (dims, ((), ())), preferred_element_type=F32)


def exchange(a, axis):
    return lax.all_to_all(a, axis, 0, 0, tiled=True)


def call(body, out, grid, in_specs, out_specs, scratch=(), flops=0, data=0, vmem=40):
    return pl.pallas_call(
        body,
        out_shape=out,
        grid=grid,
        in_specs=in_specs,
        out_specs=out_specs,
        scratch_shapes=list(scratch),
        compiler_params=pltpu.CompilerParams(vmem_limit_bytes=vmem * MIB),
        cost_estimate=pl.CostEstimate(flops=flops, bytes_accessed=data, transcendentals=0),
    )


def whole(shape):
    return pl.BlockSpec(shape, lambda *i: (0,) * len(shape))


def terms(tokens, down, up, cotangent, tasks, token_weight, pick_t, col_task, v_from, me_c, nx, nz):
    n_tok, width = tokens.shape
    cols = down.shape[1]
    sc = pick_t.shape[0]
    kv = cotangent.shape[1]
    per = 4
    steps = nx * nz // per
    blk = width // steps
    d = width // (nx * nz * 2)
    half = kv // 2
    u = half // nz
    lanes = nx * d + u

    def body(me, tok, dn, up_ref, cot, task_col, task_row, tw, pick, picked, v_ref, hidden, theirs, mine, acc, sca, low):
        i = pl.program_id(0)
        first = me[0] == 0

        @pl.when(i == 0)
        def _():
            sca[...] = (cot[...].astype(F32) * tw[...]).astype(BF)
            up_slot = dot(pick[...], up_ref[...], ((1,), (1,))).astype(BF)
            g = dot(up_slot, sca[...], ((1,), (1,)))
            low[...] = jnp.where(picked[...] == task_row[...], g, 0.0).astype(BF)

        t = tok[...]
        part = dot(t, dn[...])

        @pl.when(i == 0)
        def _():
            acc[...] = part

        @pl.when(i > 0)
        def _():
            acc[...] += part

        r = dot(low[...], t).astype(BF)
        for k in range(per):
            x, z = (i * per + k) // nz, (i * per + k) % nz
            at = pl.ds(pl.multiple_of(x * d, d), d)
            a, b = r[:, 2 * k * d : (2 * k + 1) * d], r[:, (2 * k + 1) * d : (2 * k + 2) * d]
            mine[z, :, at] = jnp.where(first, a, b)
            theirs[z, :, at] = jnp.where(first, b, a)

        @pl.when(i == steps - 1)
        def _():
            adapter = lax.broadcasted_iota(jnp.int32, (n_tok, cols), 1) // RANK
            h = jnp.where(task_col[...] == adapter, acc[...], 0.0).astype(BF)
            hidden[...] = h
            h_t = dot(pick[...], h, ((1,), (1,))).astype(BF)
            order = lax.broadcasted_iota(jnp.int32, (kv, kv), 0) == v_ref[...]
            g = dot(dot(h_t, sca[...]).astype(BF), jnp.where(order, 1.0, 0.0).astype(BF)).astype(BF)
            for k in range(nz):
                a, b = g[:, k * u : (k + 1) * u], g[:, half + k * u : half + (k + 1) * u]
                mine[k, :, nx * d :] = jnp.where(first, a, b)
                theirs[k, :, nx * d :] = jnp.where(first, b, a)

    return call(
        body,
        (
            jax.ShapeDtypeStruct((n_tok, cols), BF),
            jax.ShapeDtypeStruct((nz, sc, lanes), BF),
            jax.ShapeDtypeStruct((nz, sc, lanes), BF),
        ),
        (steps,),
        [
            pl.BlockSpec(memory_space=pltpu.SMEM),
            pl.BlockSpec((n_tok, blk), lambda i: (0, i)),
            pl.BlockSpec((blk, cols), lambda i: (i, 0)),
            whole((kv, cols)),
            whole((n_tok, kv)),
            whole((n_tok, 1)),
            whole((1, n_tok)),
            whole((n_tok, 1)),
            whole((sc, cols)),
            whole((sc, 1)),
            whole((1, kv)),
        ],
        (whole((n_tok, cols)), whole((nz, sc, lanes)), whole((nz, sc, lanes))),
        [pltpu.VMEM((n_tok, cols), F32), pltpu.VMEM((n_tok, kv), BF), pltpu.VMEM((sc, n_tok), BF)],
        flops=2 * n_tok * width * (cols + sc),
        data=24 * MIB,
        vmem=48,
    )(
        me_c,
        tokens,
        down,
        up,
        cotangent,
        tasks[:, None],
        tasks[None, :],
        token_weight,
        pick_t,
        col_task[:, None],
        v_from[None, :],
    )


def join(*lists):
    n = len(lists[0])
    rows, lanes = lists[0][0].shape

    def body(*refs):
        for k in range(len(lists)):
            for j in range(n):
                refs[n * len(lists) + k][j * rows : (j + 1) * rows] = refs[k * n + j][...]

    return call(
        body,
        tuple(jax.ShapeDtypeStruct((n * rows, lanes), BF) for _ in lists),
        (1,),
        [whole((rows, lanes))] * (n * len(lists)),
        tuple(whole((n * rows, lanes)) for _ in lists),
        data=4 * MIB,
    )(*[a for one in lists for a in one])


def halves(arrays, which):
    rows, lanes = arrays[0].shape
    steps = 2
    blk = rows // 2 // steps

    def body(*refs):
        for k in range(len(arrays)):
            refs[len(arrays) + k][...] = refs[k][...]

    return call(
        body,
        tuple(jax.ShapeDtypeStruct((rows // 2, lanes), BF) for _ in arrays),
        (steps,),
        [pl.BlockSpec((blk, lanes), lambda i, w=w: (w * steps + i, 0)) for w in which],
        tuple(pl.BlockSpec((blk, lanes), lambda i: (i, 0)) for _ in arrays),
        data=4 * MIB,
    )(*arrays)


def pack(mine, theirs, note):
    n, sc, lanes = mine.shape

    def body(a, b, c, out):
        out[0, :sc] = (a[0].astype(F32) + b[0].astype(F32)).astype(BF)
        out[0, sc:] = c[...]

    block = pl.BlockSpec((1, sc, lanes), lambda i: (i, 0, 0))
    return call(
        body,
        jax.ShapeDtypeStruct((n, sc + INFO, lanes), BF),
        (n,),
        [block, block, whole((INFO, lanes))],
        pl.BlockSpec((1, sc + INFO, lanes), lambda i: (i, 0, 0)),
        data=10 * MIB,
    )(mine, theirs, note)


def spread(got, owned_col, ny):
    n, rows, lanes = got.shape
    sc = rows - INFO
    cols = owned_col.shape[0]
    own = cols // ny

    def body(g, ow, out):
        total = jnp.zeros((own, lanes), F32)
        flag = jnp.zeros((1, lanes), BF)
        same = (
            lax.broadcasted_iota(jnp.int32, (own, sc), 0) % RANK
            == lax.broadcasted_iota(jnp.int32, (own, sc), 1) % RANK
        )
        for p in range(n):
            note = g[p, sc:, :]
            sent = note[0:1, :sc].astype(F32)
            place = jnp.where(same & (ow[...] == sent), 1.0, 0.0).astype(BF)
            total += dot(place, g[p, :sc, :])
            flag = jnp.maximum(flag, note[1:2, :])
        out[0, :own] = total.astype(BF)
        out[0, own:] = jnp.broadcast_to(flag, (INFO, lanes))

    return call(
        body,
        jax.ShapeDtypeStruct((ny, own + INFO, lanes), BF),
        (ny,),
        [whole((n, rows, lanes)), pl.BlockSpec((own, 1), lambda i: (i, 0))],
        pl.BlockSpec((1, own + INFO, lanes), lambda i: (i, 0, 0)),
        flops=2 * cols * n * sc * lanes,
        data=5 * MIB,
    )(got, owned_col)


def turn(got, nx, d):
    n, rows, lanes = got.shape
    own = rows - INFO
    v = (lanes - nx * d) // nx

    def body(g, out):
        total = g[0, :own].astype(F32)
        flag = g[0, own : own + INFO, :own]
        for p in range(1, n):
            total += g[p, :own].astype(F32)
            flag = jnp.maximum(flag, g[p, own : own + INFO, :own])
        t = total.T.astype(BF)
        for x in range(nx):
            out[x, :d] = t[x * d : (x + 1) * d]
            out[x, d : d + v] = t[nx * d + x * v : nx * d + (x + 1) * v]
            out[x, d + v :] = flag

    return call(
        body,
        jax.ShapeDtypeStruct((nx, d + v + INFO, own), BF),
        (1,),
        [whole(got.shape)],
        whole((nx, d + v + INFO, own)),
        data=2 * MIB,
    )(got)


def finish(got, d):
    n, rows, own = got.shape
    v = rows - INFO - d

    def body(g, down, up, flag):
        total = g[0].astype(F32)
        most = g[0, d + v :].astype(F32)
        for p in range(1, n):
            total += g[p].astype(F32)
            most = jnp.maximum(most, g[p, d + v :].astype(F32))
        down[...] = total[:d]
        up[...] = total[d : d + v]
        flag[...] = most

    shapes = (d, own), (v, own), (INFO, own)
    return call(
        body,
        tuple(jax.ShapeDtypeStruct(s, F32) for s in shapes),
        (1,),
        [whole(got.shape)],
        tuple(whole(s) for s in shapes),
        data=MIB // 2,
    )(got)


def shifted(a, axis, step):
    n = lax.axis_size(axis)
    return lax.ppermute(a, axis, [(i, (i + step) % n) for i in range(n)])


def add_blocks(own, other, groups, where_from, before=None, lora=None, final=False):
    n_tok = own.shape[0]
    rows = sum(w.shape[0] for w in groups[0])
    n = groups[0][0].shape[1]
    steps = len(groups)
    per = where_from.shape[0] // steps
    blk = rows // per
    flat = [w for group in groups for w in group]
    extra = [] if before is None else [before]
    if lora is not None:
        extra += list(lora)

    def body(at, *refs):
        tok_a, tok_b = refs[:per], refs[per : 2 * per]
        ws = refs[2 * per : 2 * per + len(flat)]
        more = refs[2 * per + len(flat) : 2 * per + len(flat) + len(extra)]
        outs = refs[2 * per + len(flat) + len(extra) :]
        acc = refs[-1]
        i = pl.program_id(0)

        @pl.when(i == 0)
        def _():
            if before is not None:
                acc[...] = more[0][...]
            else:
                acc[...] = jnp.zeros_like(acc)
            if lora is not None:
                h_a, h_b, u = more[-3:]
                acc[:n_tok] += SCALE * dot(h_a[...], u[...], ((1,), (1,)))
                acc[n_tok:] += SCALE * dot(h_b[...], u[...], ((1,), (1,)))

        left = 0
        for p in range(steps):
            mine = ws[left : left + len(groups[p])]
            left += len(groups[p])

            @pl.when(i == p)
            def _(mine=mine):
                parts = [w[...] for w in mine]
                w = parts[0] if len(parts) == 1 else jnp.concatenate(parts, axis=0)
                acc[:n_tok] += dot(jnp.concatenate([t[...] for t in tok_a], axis=1), w)
                acc[n_tok:] += dot(jnp.concatenate([t[...] for t in tok_b], axis=1), w)

        if final:

            @pl.when(i == steps - 1)
            def _():
                outs[0][...] = acc[:n_tok].astype(BF)
                outs[1][...] = acc[n_tok:].astype(BF)

    tok_specs = [pl.BlockSpec((n_tok, blk), lambda i, s, k=k: (0, s[i * per + k])) for k in range(per)]
    shape = (2 * n_tok, n)
    return pl.pallas_call(
        body,
        out_shape=(jax.ShapeDtypeStruct((n_tok, n), BF),) * 2 if final else jax.ShapeDtypeStruct(shape, F32),
        grid_spec=pltpu.PrefetchScalarGridSpec(
            num_scalar_prefetch=1,
            grid=(steps,),
            in_specs=tok_specs * 2 + [whole(w.shape) for w in flat] + [whole(e.shape) for e in extra],
            out_specs=(whole((n_tok, n)),) * 2 if final else whole(shape),
            scratch_shapes=[pltpu.VMEM(shape, F32)] if final else [],
        ),
        compiler_params=pltpu.CompilerParams(vmem_limit_bytes=40 * MIB),
        cost_estimate=pl.CostEstimate(
            flops=4 * n_tok * rows * n * steps, bytes_accessed=8 * n_tok * rows * steps, transcendentals=0
        ),
    )(where_from, *([own] * per), *([other] * per), *flat, *extra)


def per_device(tokens, weight, down, up, cotangent, tasks, owned, counts):
    n_tok, width = tokens.shape
    kv = weight.shape[1]
    adapters = owned.shape[0]
    cols = adapters * RANK
    ny, nx, nz = lax.axis_size("y"), lax.axis_size("x"), lax.axis_size("z")
    me_c = lax.axis_index("c")
    d_rows, v_rows = width // (nx * nz * 2), kv // (nx * nz * 2)
    me_x, me_z = lax.axis_index("x"), lax.axis_index("z")
    sc = SLOTS * RANK
    lanes = nx * (d_rows + v_rows)
    half = kv // 2

    def columns(a, core):
        return lax.dynamic_slice_in_dim(a, core * half, half, 1)

    block_a = columns(weight, me_c)
    block_b = lax.ppermute(columns(weight, 1 - me_c), "c", SWAP)
    partner_tasks = lax.ppermute(tasks, "c", SWAP)
    block_b, partner_tasks, cotangent, counts = lax.optimization_barrier((block_b, partner_tasks, cotangent, counts))
    first_hop = [shifted(block_a, "x", k) for k in range(1, nx)] + [shifted(block_b, "z", k) for k in range(1, nz)]
    def blocks_a(step):
        z = (me_z + step) % nz
        return [(((me_x - k) % nx) * nz + z) * 2 + me_c for k in range(nx)]

    def blocks_b(step):
        x = (me_x + step) % nx
        return [(x * nz + (me_z - k) % nz) * 2 + 1 - me_c for k in range(nz)]

    def at(*lists):
        return jnp.stack([i for one in lists for i in one]).astype(jnp.int32)

    ids = jnp.arange(adapters, dtype=jnp.int32)
    hit = tasks[:, None] == ids[None, :]
    present = jnp.any(hit | (partner_tasks[:, None] == ids[None, :]), axis=0)
    rank_of = jnp.sum((ids[None, :] < ids[:, None]) & present[None, :], axis=1)
    col_slot = jnp.arange(sc, dtype=jnp.int32) // RANK
    col_rank = jnp.arange(sc, dtype=jnp.int32) % RANK
    row = jnp.arange(cols, dtype=jnp.int32)

    token_count = jnp.sum(jnp.where(hit, counts.astype(F32)[None, :], 0.0), axis=1)
    token_weight = (SCALE / token_count)[:, None]
    v_out = jnp.arange(kv, dtype=jnp.int32)
    v_from = (
        (v_out // v_rows % nx) * (nz * 2 * v_rows)
        + (v_out // (v_rows * nx) % nz) * (2 * v_rows)
        + v_out // (v_rows * nx * nz) * v_rows
        + v_out % v_rows
    )

    owned_col = jnp.repeat(owned.astype(F32), RANK)[:, None]

    def local_terms(first):
        chosen = present[None, :] & (rank_of[None, :] == first + col_slot[:, None])
        col_task = jnp.sum(jnp.where(chosen, ids[None, :] + 1, 0), axis=1) - 1
        more = (jnp.sum(present.astype(jnp.int32)) > first + SLOTS).astype(F32)
        pick_t = ((row // RANK)[None, :] == col_task[:, None]) & ((row % RANK)[None, :] == col_rank[:, None])
        pick_t = pick_t.astype(BF)
        hidden, theirs, mine = terms(
            tokens,
            down,
            up,
            cotangent,
            tasks,
            token_weight,
            pick_t,
            col_task,
            v_from,
            me_c.astype(jnp.int32)[None],
            nx,
            nz,
        )
        note_row = lax.broadcasted_iota(jnp.int32, (INFO, lanes), 0)
        note = jnp.where(note_row == 0, jnp.pad(col_task.astype(F32), (0, lanes - sc))[None, :], more)
        return hidden, theirs, mine, note.astype(BF)

    hidden, theirs, mine, note = local_terms(jnp.int32(0))
    first_hop, theirs = lax.optimization_barrier((first_hop, theirs))
    got = lax.ppermute(theirs, "c", SWAP)
    near_a, near_b = join([block_a] + first_hop[: nx - 1], [block_b] + first_hop[nx - 1 :])
    a_down, a_up = shifted(near_a, "z", 1), shifted(near_a, "z", nz - 1)
    b_down, b_up = shifted(near_b, "x", 1), shifted(near_b, "x", nx - 1)
    pass_on = halves([a_down, a_up, b_down, b_up], [0, 1, 0, 1])
    a_far = [shifted(pass_on[0], "z", 1), shifted(pass_on[1], "z", nz - 1)]
    b_far = [shifted(pass_on[2], "x", 1), shifted(pass_on[3], "x", nx - 1)]

    from_z = exchange(pack(mine, got, note), "z")

    sent_tokens, sent_hidden, _ = lax.optimization_barrier((tokens, hidden, got))
    other = lax.ppermute(sent_tokens, "c", SWAP)
    other_hidden = lax.ppermute(sent_hidden, "c", SWAP)
    acc = add_blocks(tokens, other, [[near_a], [near_b]], at(blocks_a(0), blocks_b(0)))
    from_z, acc = lax.optimization_barrier((from_z, acc))
    from_y = exchange(spread(from_z, owned_col, ny), "y")
    by_x = turn(from_y, nx, d_rows)
    by_x, acc = lax.optimization_barrier((by_x, acc))
    grad_down, grad_up, flags = finish(exchange(by_x, "x"), d_rows)
    acc = add_blocks(
        tokens,
        other,
        [[a_down], [a_up], [b_down], [b_up]],
        at(blocks_a(-1), blocks_a(1), blocks_b(-1), blocks_b(1)),
        before=acc,
        lora=(hidden, other_hidden, lax.dynamic_slice_in_dim(up, me_c * half, half, 0)),
    )
    acc, flags = lax.optimization_barrier((acc, flags))
    tile, sent = add_blocks(tokens, other, [a_far, b_far], at(blocks_a(2), blocks_b(2)), before=acc, final=True)
    back = lax.ppermute(sent, "c", SWAP)
    keys = jnp.concatenate([jnp.where(me_c == 0, tile, back), jnp.where(me_c == 0, back, tile)], axis=1)

    flag, keys = lax.optimization_barrier((flags[0, 0], keys))

    def again(state):
        first, down_sum, up_sum, _ = state
        _, theirs, mine, note = local_terms(first)
        by_owner = spread(exchange(pack(mine, lax.ppermute(theirs, "c", SWAP), note), "z"), owned_col, ny)
        by_x = turn(exchange(by_owner, "y"), nx, d_rows)
        down_more, up_more, flags = finish(exchange(by_x, "x"), d_rows)
        return first + SLOTS, down_sum + down_more, up_sum + up_more, flags[0, 0]

    _, grad_down, grad_up, _ = lax.while_loop(
        lambda state: state[3] > 0.5, again, (jnp.int32(SLOTS), grad_down, grad_up, flag)
    )
    return keys, grad_down[None], grad_up[None]


def solution(mesh):
    sizes = dict(mesh.shape)
    ny = sizes["grp"]
    nx = nz = int((sizes["fsdp"] // 2) ** 0.5)
    fine = Mesh(mesh.devices.reshape(ny, nx, nz, 2), ("y", "x", "z", "c"))
    fsdp = ("x", "z", "c")
    every = ("y", "x", "z", "c")
    in_specs = (P(every, None), P(fsdp, None), P(), P(), P(every, None), P(every), P(), P())
    out_specs = (P(every, None), P("y", fsdp, None), P("y", fsdp, None))
    return jax.shard_map(per_device, mesh=fine, in_specs=in_specs, out_specs=out_specs, check_vma=False)
```

```python
import jax
import jax.numpy as jnp
from jax import lax
from jax.experimental import pallas as pl
from jax.experimental.pallas import tpu as pltpu
from jax.sharding import Mesh, PartitionSpec as P

RANK = 64
SCALE = 0.5
BF = jnp.bfloat16
F32 = jnp.float32
SLOTS = 2
INFO = 16
MIB = 1 << 20
SWAP = [(0, 1), (1, 0)]


def dot(a, b, dims=((1,), (0,))):
    return lax.dot_general(a, b, (dims, ((), ())), preferred_element_type=F32)


def exchange(a, axis):
    return lax.all_to_all(a, axis, 0, 0, tiled=True)


def call(body, out, grid, in_specs, out_specs, scratch=(), flops=0, data=0, vmem=12):
    return pl.pallas_call(
        body,
        out_shape=out,
        grid=grid,
        in_specs=in_specs,
        out_specs=out_specs,
        scratch_shapes=list(scratch),
        compiler_params=pltpu.CompilerParams(vmem_limit_bytes=vmem * MIB),
        cost_estimate=pl.CostEstimate(flops=flops, bytes_accessed=data, transcendentals=0),
    )


def whole(shape):
    return pl.BlockSpec(shape, lambda *i: (0,) * len(shape))


def once(shape):
    return pl.BlockSpec(shape, lambda *i: (0,) * len(shape), pipeline_mode=pl.Buffered(1))


def terms(tokens, down, up, cotangent, tasks, token_weight, pick_t, col_task, v_from, me_c, nx, nz):
    n_tok, width = tokens.shape
    cols = down.shape[1]
    sc = pick_t.shape[0]
    kv = cotangent.shape[1]
    per = 4
    steps = nx * nz // per
    blk = width // steps
    d = width // (nx * nz * 2)
    half = kv // 2
    u = half // nz
    lanes = nx * d + u

    def body(me, tok, dn, up_ref, cot, task_col, task_row, tw, pick, picked, v_ref, hidden, theirs, mine, acc, sca, low):
        i = pl.program_id(0)
        first = me[0] == 0

        @pl.when(i == 0)
        def _():
            sca[...] = (cot[...].astype(F32) * tw[...]).astype(BF)
            up_slot = dot(pick[...], up_ref[...], ((1,), (1,))).astype(BF)
            g = dot(up_slot, sca[...], ((1,), (1,)))
            low[...] = jnp.where(picked[...] == task_row[...], g, 0.0).astype(BF)

        t = tok[...]
        part = dot(t, dn[...])

        @pl.when(i == 0)
        def _():
            acc[...] = part

        @pl.when(i > 0)
        def _():
            acc[...] += part

        r = dot(low[...], t).astype(BF)
        for k in range(per):
            x, z = (i * per + k) // nz, (i * per + k) % nz
            at = pl.ds(pl.multiple_of(x * d, d), d)
            a, b = r[:, 2 * k * d : (2 * k + 1) * d], r[:, (2 * k + 1) * d : (2 * k + 2) * d]
            mine[z, :, at] = jnp.where(first, a, b)
            theirs[z, :, at] = jnp.where(first, b, a)

        @pl.when(i == steps - 1)
        def _():
            adapter = lax.broadcasted_iota(jnp.int32, (n_tok, cols), 1) // RANK
            h = jnp.where(task_col[...] == adapter, acc[...], 0.0).astype(BF)
            hidden[...] = h
            h_t = dot(pick[...], h, ((1,), (1,))).astype(BF)
            order = lax.broadcasted_iota(jnp.int32, (kv, kv), 0) == v_ref[...]
            g = dot(dot(h_t, sca[...]).astype(BF), jnp.where(order, 1.0, 0.0).astype(BF)).astype(BF)
            for k in range(nz):
                a, b = g[:, k * u : (k + 1) * u], g[:, half + k * u : half + (k + 1) * u]
                mine[k, :, nx * d :] = jnp.where(first, a, b)
                theirs[k, :, nx * d :] = jnp.where(first, b, a)

    return call(
        body,
        (
            jax.ShapeDtypeStruct((n_tok, cols), BF),
            jax.ShapeDtypeStruct((nz, sc, lanes), BF),
            jax.ShapeDtypeStruct((nz, sc, lanes), BF),
        ),
        (steps,),
        [
            pl.BlockSpec(memory_space=pltpu.SMEM),
            pl.BlockSpec((n_tok, blk), lambda i: (0, i)),
            pl.BlockSpec((blk, cols), lambda i: (i, 0)),
            once((kv, cols)),
            once((n_tok, kv)),
            once((n_tok, 1)),
            once((1, n_tok)),
            once((n_tok, 1)),
            once((sc, cols)),
            once((sc, 1)),
            once((1, kv)),
        ],
        (whole((n_tok, cols)), whole((nz, sc, lanes)), whole((nz, sc, lanes))),
        [pltpu.VMEM((n_tok, cols), F32), pltpu.VMEM((n_tok, kv), BF), pltpu.VMEM((sc, n_tok), BF)],
        flops=2 * n_tok * width * (cols + sc),
        data=24 * MIB,
        vmem=28,
    )(
        me_c,
        tokens,
        down,
        up,
        cotangent,
        tasks[:, None],
        tasks[None, :],
        token_weight,
        pick_t,
        col_task[:, None],
        v_from[None, :],
    )


def join(*lists):
    n = len(lists[0])
    rows, lanes = lists[0][0].shape

    def body(*refs):
        for k in range(len(lists)):
            for j in range(n):
                refs[n * len(lists) + k][j * rows : (j + 1) * rows] = refs[k * n + j][...]

    return call(
        body,
        tuple(jax.ShapeDtypeStruct((n * rows, lanes), BF) for _ in lists),
        (1,),
        [once((rows, lanes))] * (n * len(lists)),
        tuple(whole((n * rows, lanes)) for _ in lists),
        data=4 * MIB,
    )(*[a for one in lists for a in one])


def halves(arrays, which):
    rows, lanes = arrays[0].shape
    steps = 2
    blk = rows // 2 // steps

    def body(*refs):
        for k in range(len(arrays)):
            refs[len(arrays) + k][...] = refs[k][...]

    return call(
        body,
        tuple(jax.ShapeDtypeStruct((rows // 2, lanes), BF) for _ in arrays),
        (steps,),
        [pl.BlockSpec((blk, lanes), lambda i, w=w: (w * steps + i, 0)) for w in which],
        tuple(pl.BlockSpec((blk, lanes), lambda i: (i, 0)) for _ in arrays),
        data=4 * MIB,
    )(*arrays)


def pack(mine, theirs, note):
    n, sc, lanes = mine.shape

    def body(a, b, c, out):
        out[0, :sc] = (a[0].astype(F32) + b[0].astype(F32)).astype(BF)
        out[0, sc:] = c[...]

    block = pl.BlockSpec((1, sc, lanes), lambda i: (i, 0, 0))
    return call(
        body,
        jax.ShapeDtypeStruct((n, sc + INFO, lanes), BF),
        (n,),
        [block, block, whole((INFO, lanes))],
        pl.BlockSpec((1, sc + INFO, lanes), lambda i: (i, 0, 0)),
        data=10 * MIB,
    )(mine, theirs, note)


def spread(got, owned_col, ny):
    n, rows, lanes = got.shape
    sc = rows - INFO
    cols = owned_col.shape[0]
    own = cols // ny

    def body(g, ow, out):
        total = jnp.zeros((own, lanes), F32)
        flag = jnp.zeros((1, lanes), BF)
        same = (
            lax.broadcasted_iota(jnp.int32, (own, sc), 0) % RANK
            == lax.broadcasted_iota(jnp.int32, (own, sc), 1) % RANK
        )
        for p in range(n):
            note = g[p, sc:, :]
            sent = note[0:1, :sc].astype(F32)
            place = jnp.where(same & (ow[...] == sent), 1.0, 0.0).astype(BF)
            total += dot(place, g[p, :sc, :])
            flag = jnp.maximum(flag, note[1:2, :])
        out[0, :own] = total.astype(BF)
        out[0, own:] = jnp.broadcast_to(flag, (INFO, lanes))

    return call(
        body,
        jax.ShapeDtypeStruct((ny, own + INFO, lanes), BF),
        (ny,),
        [once((n, rows, lanes)), pl.BlockSpec((own, 1), lambda i: (i, 0))],
        pl.BlockSpec((1, own + INFO, lanes), lambda i: (i, 0, 0)),
        flops=2 * cols * n * sc * lanes,
        data=5 * MIB,
    )(got, owned_col)


def turn(got, nx, d):
    n, rows, lanes = got.shape
    own = rows - INFO
    v = (lanes - nx * d) // nx

    def body(g, out):
        total = g[0, :own].astype(F32)
        flag = g[0, own : own + INFO, :own]
        for p in range(1, n):
            total += g[p, :own].astype(F32)
            flag = jnp.maximum(flag, g[p, own : own + INFO, :own])
        t = total.T.astype(BF)
        for x in range(nx):
            out[x, :d] = t[x * d : (x + 1) * d]
            out[x, d : d + v] = t[nx * d + x * v : nx * d + (x + 1) * v]
            out[x, d + v :] = flag

    return call(
        body,
        jax.ShapeDtypeStruct((nx, d + v + INFO, own), BF),
        (1,),
        [whole(got.shape)],
        whole((nx, d + v + INFO, own)),
        data=2 * MIB,
    )(got)


def finish(got, d):
    n, rows, own = got.shape
    v = rows - INFO - d

    def body(g, down, up, flag):
        total = g[0].astype(F32)
        most = g[0, d + v :].astype(F32)
        for p in range(1, n):
            total += g[p].astype(F32)
            most = jnp.maximum(most, g[p, d + v :].astype(F32))
        down[...] = total[:d]
        up[...] = total[d : d + v]
        flag[...] = most

    shapes = (d, own), (v, own), (INFO, own)
    return call(
        body,
        tuple(jax.ShapeDtypeStruct(s, F32) for s in shapes),
        (1,),
        [whole(got.shape)],
        tuple(whole(s) for s in shapes),
        data=MIB // 2,
    )(got)


def shifted(a, axis, step):
    n = lax.axis_size(axis)
    return lax.ppermute(a, axis, [(i, (i + step) % n) for i in range(n)])


def add_blocks(own, other, groups, where_from, before=None, lora=None, final=False):
    n_tok = own.shape[0]
    rows = sum(w.shape[0] for w in groups[0])
    n = groups[0][0].shape[1]
    steps = len(groups)
    per = where_from.shape[0] // steps
    blk = rows // per
    flat = [w for group in groups for w in group]
    extra = [] if before is None else [before]
    extra_specs = [once(e.shape) for e in extra]
    if lora is not None:
        extra += list(lora)
        extra_specs += [once(e.shape) for e in lora[:2]]
        extra_specs.append(pl.BlockSpec((n, lora[2].shape[1]), lambda i, s: (s[steps * per], 0)))

    def body(at, *refs):
        tok_a, tok_b = refs[:per], refs[per : 2 * per]
        ws = refs[2 * per : 2 * per + len(flat)]
        more = refs[2 * per + len(flat) : 2 * per + len(flat) + len(extra)]
        outs = refs[2 * per + len(flat) + len(extra) :]
        acc = refs[-1]
        i = pl.program_id(0)

        @pl.when(i == 0)
        def _():
            if before is not None:
                acc[...] = more[0][...]
            else:
                acc[...] = jnp.zeros_like(acc)
            if lora is not None:
                h_a, h_b, u = more[-3:]
                acc[:n_tok] += SCALE * dot(h_a[...], u[...], ((1,), (1,)))
                acc[n_tok:] += SCALE * dot(h_b[...], u[...], ((1,), (1,)))

        left = 0
        for p in range(steps):
            mine = ws[left : left + len(groups[p])]
            left += len(groups[p])

            @pl.when(i == p)
            def _(mine=mine):
                parts = [w[...] for w in mine]
                w = parts[0] if len(parts) == 1 else jnp.concatenate(parts, axis=0)
                acc[:n_tok] += dot(jnp.concatenate([t[...] for t in tok_a], axis=1), w)
                acc[n_tok:] += dot(jnp.concatenate([t[...] for t in tok_b], axis=1), w)

        if final:

            @pl.when(i == steps - 1)
            def _():
                outs[0][...] = acc[:n_tok].astype(BF)
                outs[1][...] = acc[n_tok:].astype(BF)

    tok_specs = [pl.BlockSpec((n_tok, blk), lambda i, s, k=k: (0, s[i * per + k])) for k in range(per)]
    shape = (2 * n_tok, n)
    return pl.pallas_call(
        body,
        out_shape=(jax.ShapeDtypeStruct((n_tok, n), BF),) * 2 if final else jax.ShapeDtypeStruct(shape, F32),
        grid_spec=pltpu.PrefetchScalarGridSpec(
            num_scalar_prefetch=1,
            grid=(steps,),
            in_specs=tok_specs * 2 + [once(w.shape) for w in flat] + extra_specs,
            out_specs=(whole((n_tok, n)),) * 2 if final else whole(shape),
            scratch_shapes=[pltpu.VMEM(shape, F32)] if final else [],
        ),
        compiler_params=pltpu.CompilerParams(vmem_limit_bytes=22 * MIB),
        cost_estimate=pl.CostEstimate(
            flops=4 * n_tok * rows * n * steps, bytes_accessed=8 * n_tok * rows * steps, transcendentals=0
        ),
    )(where_from, *([own] * per), *([other] * per), *flat, *extra)


def per_device(tokens, weight, down, up, cotangent, tasks, owned, counts):
    n_tok, width = tokens.shape
    kv = weight.shape[1]
    adapters = owned.shape[0]
    cols = adapters * RANK
    ny, nx, nz = lax.axis_size("y"), lax.axis_size("x"), lax.axis_size("z")
    me_c = lax.axis_index("c")
    d_rows, v_rows = width // (nx * nz * 2), kv // (nx * nz * 2)
    me_x, me_z = lax.axis_index("x"), lax.axis_index("z")
    sc = SLOTS * RANK
    lanes = nx * (d_rows + v_rows)
    half = kv // 2

    def columns(a, core):
        return lax.dynamic_slice_in_dim(a, core * half, half, 1)

    block_a = columns(weight, me_c)
    block_b = lax.ppermute(columns(weight, 1 - me_c), "c", SWAP)
    partner_tasks = lax.ppermute(tasks, "c", SWAP)
    block_b, partner_tasks, cotangent, counts = lax.optimization_barrier((block_b, partner_tasks, cotangent, counts))
    first_hop = [shifted(block_a, "x", k) for k in range(1, nx)] + [shifted(block_b, "z", k) for k in range(1, nz)]
    def blocks_a(step):
        z = (me_z + step) % nz
        return [(((me_x - k) % nx) * nz + z) * 2 + me_c for k in range(nx)]

    def blocks_b(step):
        x = (me_x + step) % nx
        return [(x * nz + (me_z - k) % nz) * 2 + 1 - me_c for k in range(nz)]

    def at(*lists):
        return jnp.stack([i for one in lists for i in one]).astype(jnp.int32)

    ids = jnp.arange(adapters, dtype=jnp.int32)
    hit = tasks[:, None] == ids[None, :]
    present = jnp.any(hit | (partner_tasks[:, None] == ids[None, :]), axis=0)
    rank_of = jnp.sum((ids[None, :] < ids[:, None]) & present[None, :], axis=1)
    col_slot = jnp.arange(sc, dtype=jnp.int32) // RANK
    col_rank = jnp.arange(sc, dtype=jnp.int32) % RANK
    row = jnp.arange(cols, dtype=jnp.int32)

    token_count = jnp.sum(jnp.where(hit, counts.astype(F32)[None, :], 0.0), axis=1)
    token_weight = (SCALE / token_count)[:, None]
    v_out = jnp.arange(kv, dtype=jnp.int32)
    v_from = (
        (v_out // v_rows % nx) * (nz * 2 * v_rows)
        + (v_out // (v_rows * nx) % nz) * (2 * v_rows)
        + v_out // (v_rows * nx * nz) * v_rows
        + v_out % v_rows
    )

    owned_col = jnp.repeat(owned.astype(F32), RANK)[:, None]

    def local_terms(first):
        chosen = present[None, :] & (rank_of[None, :] == first + col_slot[:, None])
        col_task = jnp.sum(jnp.where(chosen, ids[None, :] + 1, 0), axis=1) - 1
        more = (jnp.sum(present.astype(jnp.int32)) > first + SLOTS).astype(F32)
        pick_t = ((row // RANK)[None, :] == col_task[:, None]) & ((row % RANK)[None, :] == col_rank[:, None])
        pick_t = pick_t.astype(BF)
        hidden, theirs, mine = terms(
            tokens,
            down,
            up,
            cotangent,
            tasks,
            token_weight,
            pick_t,
            col_task,
            v_from,
            me_c.astype(jnp.int32)[None],
            nx,
            nz,
        )
        note_row = lax.broadcasted_iota(jnp.int32, (INFO, lanes), 0)
        note = jnp.where(note_row == 0, jnp.pad(col_task.astype(F32), (0, lanes - sc))[None, :], more)
        return hidden, theirs, mine, note.astype(BF)

    hidden, theirs, mine, note = local_terms(jnp.int32(0))
    first_hop, theirs = lax.optimization_barrier((first_hop, theirs))
    near_a, near_b = join([block_a] + first_hop[: nx - 1], [block_b] + first_hop[nx - 1 :])
    near_a, near_b, theirs = lax.optimization_barrier((near_a, near_b, theirs))
    got = lax.ppermute(theirs, "c", SWAP)
    a_down, a_up = shifted(near_a, "z", 1), shifted(near_a, "z", nz - 1)
    b_down, b_up = shifted(near_b, "x", 1), shifted(near_b, "x", nx - 1)
    pass_on = halves([a_down, a_up, b_down, b_up], [0, 1, 0, 1])
    a_far = [shifted(pass_on[0], "z", 1), shifted(pass_on[1], "z", nz - 1)]
    b_far = [shifted(pass_on[2], "x", 1), shifted(pass_on[3], "x", nx - 1)]

    from_z = exchange(pack(mine, got, note), "z")

    sent_tokens, sent_hidden, _ = lax.optimization_barrier((tokens, hidden, got))
    other = lax.ppermute(sent_tokens, "c", SWAP)
    other_hidden = lax.ppermute(sent_hidden, "c", SWAP)
    acc = add_blocks(
        tokens,
        other,
        [[near_a], [near_b]],
        at(blocks_a(0), blocks_b(0), [me_c]),
        lora=(hidden, other_hidden, up),
    )
    from_z, acc = lax.optimization_barrier((from_z, acc))
    from_y = exchange(spread(from_z, owned_col, ny), "y")
    by_x = turn(from_y, nx, d_rows)
    by_x, acc = lax.optimization_barrier((by_x, acc))
    grad_down, grad_up, flags = finish(exchange(by_x, "x"), d_rows)
    acc = add_blocks(
        tokens,
        other,
        [[a_down], [a_up], [b_down], [b_up]],
        at(blocks_a(-1), blocks_a(1), blocks_b(-1), blocks_b(1)),
        before=acc,
    )
    acc, flags = lax.optimization_barrier((acc, flags))
    tile, sent = add_blocks(tokens, other, [a_far, b_far], at(blocks_a(2), blocks_b(2)), before=acc, final=True)
    back = lax.ppermute(sent, "c", SWAP)
    keys = jnp.concatenate([jnp.where(me_c == 0, tile, back), jnp.where(me_c == 0, back, tile)], axis=1)

    flag, keys = lax.optimization_barrier((flags[0, 0], keys))

    def again(state):
        first, down_sum, up_sum, _ = state
        _, theirs, mine, note = local_terms(first)
        by_owner = spread(exchange(pack(mine, lax.ppermute(theirs, "c", SWAP), note), "z"), owned_col, ny)
        by_x = turn(exchange(by_owner, "y"), nx, d_rows)
        down_more, up_more, flags = finish(exchange(by_x, "x"), d_rows)
        return first + SLOTS, down_sum + down_more, up_sum + up_more, flags[0, 0]

    _, grad_down, grad_up, _ = lax.while_loop(
        lambda state: state[3] > 0.5, again, (jnp.int32(SLOTS), grad_down, grad_up, flag)
    )
    return keys, grad_down[None], grad_up[None]


def solution(mesh):
    sizes = dict(mesh.shape)
    ny = sizes["grp"]
    nx = nz = int((sizes["fsdp"] // 2) ** 0.5)
    fine = Mesh(mesh.devices.reshape(ny, nx, nz, 2), ("y", "x", "z", "c"))
    fsdp = ("x", "z", "c")
    every = ("y", "x", "z", "c")
    in_specs = (P(every, None), P(fsdp, None), P(), P(), P(every, None), P(every), P(), P())
    out_specs = (P(every, None), P("y", fsdp, None), P("y", fsdp, None))
    return jax.shard_map(per_device, mesh=fine, in_specs=in_specs, out_specs=out_specs, check_vma=False)
```

```python
import jax
import jax.numpy as jnp
from jax import lax
from jax.experimental import pallas as pl
from jax.experimental.pallas import tpu as pltpu
from jax.sharding import Mesh, PartitionSpec as P

RANK = 64
SCALE = 0.5
BF = jnp.bfloat16
F32 = jnp.float32
SLOTS = 2
INFO = 16
MIB = 1 << 20
SWAP = [(0, 1), (1, 0)]


def dot(a, b, dims=((1,), (0,))):
    return lax.dot_general(a, b, (dims, ((), ())), preferred_element_type=F32)


def exchange(a, axis):
    return lax.all_to_all(a, axis, 0, 0, tiled=True)


def call(body, out, grid, in_specs, out_specs, scratch=(), flops=0, data=0, vmem=12):
    return pl.pallas_call(
        body,
        out_shape=out,
        grid=grid,
        in_specs=in_specs,
        out_specs=out_specs,
        scratch_shapes=list(scratch),
        compiler_params=pltpu.CompilerParams(vmem_limit_bytes=vmem * MIB),
        cost_estimate=pl.CostEstimate(flops=flops, bytes_accessed=data, transcendentals=0),
    )


def whole(shape):
    return pl.BlockSpec(shape, lambda *i: (0,) * len(shape))


def once(shape):
    return pl.BlockSpec(shape, lambda *i: (0,) * len(shape), pipeline_mode=pl.Buffered(1))


def terms(tokens, down, up, cotangent, tasks, token_weight, pick_t, col_task, v_from, me_c, nx, nz):
    n_tok, width = tokens.shape
    cols = down.shape[1]
    sc = pick_t.shape[0]
    kv = cotangent.shape[1]
    per = 4
    steps = nx * nz // per
    blk = width // steps
    d = width // (nx * nz * 2)
    half = kv // 2
    u = half // nz
    lanes = nx * d + u

    def body(me, tok, dn, up_ref, cot, task_col, task_row, tw, pick, picked, v_ref, hidden, theirs, mine, acc, sca, low):
        i = pl.program_id(0)
        first = me[0] == 0

        @pl.when(i == 0)
        def _():
            sca[...] = (cot[...].astype(F32) * tw[...]).astype(BF)
            up_slot = dot(pick[...], up_ref[...], ((1,), (1,))).astype(BF)
            g = dot(up_slot, sca[...], ((1,), (1,)))
            low[...] = jnp.where(picked[...] == task_row[...], g, 0.0).astype(BF)

        t = tok[...]
        part = dot(t, dn[...])

        @pl.when(i == 0)
        def _():
            acc[...] = part

        @pl.when(i > 0)
        def _():
            acc[...] += part

        r = dot(low[...], t).astype(BF)
        for k in range(per):
            x, z = (i * per + k) // nz, (i * per + k) % nz
            at = pl.ds(pl.multiple_of(x * d, d), d)
            a, b = r[:, 2 * k * d : (2 * k + 1) * d], r[:, (2 * k + 1) * d : (2 * k + 2) * d]
            mine[z, :, at] = jnp.where(first, a, b)
            theirs[z, :, at] = jnp.where(first, b, a)

        @pl.when(i == steps - 1)
        def _():
            adapter = lax.broadcasted_iota(jnp.int32, (n_tok, cols), 1) // RANK
            h = jnp.where(task_col[...] == adapter, acc[...], 0.0).astype(BF)
            hidden[...] = h
            h_t = dot(pick[...], h, ((1,), (1,))).astype(BF)
            order = lax.broadcasted_iota(jnp.int32, (kv, kv), 0) == v_ref[...]
            g = dot(dot(h_t, sca[...]).astype(BF), jnp.where(order, 1.0, 0.0).astype(BF)).astype(BF)
            for k in range(nz):
                a, b = g[:, k * u : (k + 1) * u], g[:, half + k * u : half + (k + 1) * u]
                mine[k, :, nx * d :] = jnp.where(first, a, b)
                theirs[k, :, nx * d :] = jnp.where(first, b, a)

    return call(
        body,
        (
            jax.ShapeDtypeStruct((n_tok, cols), BF),
            jax.ShapeDtypeStruct((nz, sc, lanes), BF),
            jax.ShapeDtypeStruct((nz, sc, lanes), BF),
        ),
        (steps,),
        [
            pl.BlockSpec(memory_space=pltpu.SMEM),
            pl.BlockSpec((n_tok, blk), lambda i: (0, i)),
            pl.BlockSpec((blk, cols), lambda i: (i, 0)),
            once((kv, cols)),
            once((n_tok, kv)),
            once((n_tok, 1)),
            once((1, n_tok)),
            once((n_tok, 1)),
            once((sc, cols)),
            once((sc, 1)),
            once((1, kv)),
        ],
        (whole((n_tok, cols)), whole((nz, sc, lanes)), whole((nz, sc, lanes))),
        [pltpu.VMEM((n_tok, cols), F32), pltpu.VMEM((n_tok, kv), BF), pltpu.VMEM((sc, n_tok), BF)],
        flops=2 * n_tok * width * (cols + sc),
        data=24 * MIB,
        vmem=28,
    )(
        me_c,
        tokens,
        down,
        up,
        cotangent,
        tasks[:, None],
        tasks[None, :],
        token_weight,
        pick_t,
        col_task[:, None],
        v_from[None, :],
    )


def join(*lists):
    n = len(lists[0])
    rows, lanes = lists[0][0].shape

    def body(*refs):
        for k in range(len(lists)):
            for j in range(n):
                refs[n * len(lists) + k][j * rows : (j + 1) * rows] = refs[k * n + j][...]

    return call(
        body,
        tuple(jax.ShapeDtypeStruct((n * rows, lanes), BF) for _ in lists),
        (1,),
        [once((rows, lanes))] * (n * len(lists)),
        tuple(whole((n * rows, lanes)) for _ in lists),
        data=4 * MIB,
    )(*[a for one in lists for a in one])


def halves(arrays, which):
    rows, lanes = arrays[0].shape
    steps = 2
    blk = rows // 2 // steps

    def body(*refs):
        for k in range(len(arrays)):
            refs[len(arrays) + k][...] = refs[k][...]

    return call(
        body,
        tuple(jax.ShapeDtypeStruct((rows // 2, lanes), BF) for _ in arrays),
        (steps,),
        [pl.BlockSpec((blk, lanes), lambda i, w=w: (w * steps + i, 0)) for w in which],
        tuple(pl.BlockSpec((blk, lanes), lambda i: (i, 0)) for _ in arrays),
        data=4 * MIB,
    )(*arrays)


def pack(mine, theirs, note):
    n, sc, lanes = mine.shape

    def body(a, b, c, out):
        out[0, :sc] = (a[0].astype(F32) + b[0].astype(F32)).astype(BF)
        out[0, sc:] = c[...]

    block = pl.BlockSpec((1, sc, lanes), lambda i: (i, 0, 0))
    return call(
        body,
        jax.ShapeDtypeStruct((n, sc + INFO, lanes), BF),
        (n,),
        [block, block, whole((INFO, lanes))],
        pl.BlockSpec((1, sc + INFO, lanes), lambda i: (i, 0, 0)),
        data=10 * MIB,
    )(mine, theirs, note)


def spread(got, owned_col, ny):
    n, rows, lanes = got.shape
    sc = rows - INFO
    cols = owned_col.shape[0]
    own = cols // ny

    def body(g, ow, out):
        total = jnp.zeros((own, lanes), F32)
        flag = jnp.zeros((1, lanes), BF)
        same = (
            lax.broadcasted_iota(jnp.int32, (own, sc), 0) % RANK
            == lax.broadcasted_iota(jnp.int32, (own, sc), 1) % RANK
        )
        for p in range(n):
            note = g[p, sc:, :]
            sent = note[0:1, :sc].astype(F32)
            place = jnp.where(same & (ow[...] == sent), 1.0, 0.0).astype(BF)
            total += dot(place, g[p, :sc, :])
            flag = jnp.maximum(flag, note[1:2, :])
        out[0, :own] = total.astype(BF)
        out[0, own:] = jnp.broadcast_to(flag, (INFO, lanes))

    return call(
        body,
        jax.ShapeDtypeStruct((ny, own + INFO, lanes), BF),
        (ny,),
        [once((n, rows, lanes)), pl.BlockSpec((own, 1), lambda i: (i, 0))],
        pl.BlockSpec((1, own + INFO, lanes), lambda i: (i, 0, 0)),
        flops=2 * cols * n * sc * lanes,
        data=5 * MIB,
    )(got, owned_col)


def turn(got, nx, d):
    n, rows, lanes = got.shape
    own = rows - INFO
    v = (lanes - nx * d) // nx

    def body(g, out):
        total = g[0, :own].astype(F32)
        flag = g[0, own : own + INFO, :own]
        for p in range(1, n):
            total += g[p, :own].astype(F32)
            flag = jnp.maximum(flag, g[p, own : own + INFO, :own])
        t = total.T.astype(BF)
        for x in range(nx):
            out[x, :d] = t[x * d : (x + 1) * d]
            out[x, d : d + v] = t[nx * d + x * v : nx * d + (x + 1) * v]
            out[x, d + v :] = flag

    return call(
        body,
        jax.ShapeDtypeStruct((nx, d + v + INFO, own), BF),
        (1,),
        [whole(got.shape)],
        whole((nx, d + v + INFO, own)),
        data=2 * MIB,
    )(got)


def finish(got, d):
    n, rows, own = got.shape
    v = rows - INFO - d

    def body(g, down, up, flag):
        total = g[0].astype(F32)
        most = g[0, d + v :].astype(F32)
        for p in range(1, n):
            total += g[p].astype(F32)
            most = jnp.maximum(most, g[p, d + v :].astype(F32))
        down[...] = total[:d]
        up[...] = total[d : d + v]
        flag[...] = most

    shapes = (d, own), (v, own), (INFO, own)
    return call(
        body,
        tuple(jax.ShapeDtypeStruct(s, F32) for s in shapes),
        (1,),
        [whole(got.shape)],
        tuple(whole(s) for s in shapes),
        data=MIB // 2,
    )(got)


def shifted(a, axis, step):
    n = lax.axis_size(axis)
    return lax.ppermute(a, axis, [(i, (i + step) % n) for i in range(n)])


def add_blocks(own, other, groups, where_from, before=None, lora=None, final=False):
    n_tok = own.shape[0]
    rows = sum(w.shape[0] for w in groups[0])
    n = groups[0][0].shape[1]
    steps = len(groups)
    per = where_from.shape[0] // steps
    blk = rows // per
    flat = [w for group in groups for w in group]
    extra = [] if before is None else [before]
    extra_specs = [once(e.shape) for e in extra]
    if lora is not None:
        extra += list(lora)
        extra_specs += [once(e.shape) for e in lora[:2]]
        extra_specs.append(pl.BlockSpec((n, lora[2].shape[1]), lambda i, s: (s[steps * per], 0)))

    def body(at, *refs):
        tok_a, tok_b = refs[:per], refs[per : 2 * per]
        ws = refs[2 * per : 2 * per + len(flat)]
        more = refs[2 * per + len(flat) : 2 * per + len(flat) + len(extra)]
        outs = refs[2 * per + len(flat) + len(extra) :]
        acc = refs[-1]
        i = pl.program_id(0)

        @pl.when(i == 0)
        def _():
            if before is not None:
                acc[...] = more[0][...]
            else:
                acc[...] = jnp.zeros_like(acc)
            if lora is not None:
                h_a, h_b, u = more[-3:]
                acc[:n_tok] += SCALE * dot(h_a[...], u[...], ((1,), (1,)))
                acc[n_tok:] += SCALE * dot(h_b[...], u[...], ((1,), (1,)))

        left = 0
        for p in range(steps):
            mine = ws[left : left + len(groups[p])]
            left += len(groups[p])

            @pl.when(i == p)
            def _(mine=mine):
                parts = [w[...] for w in mine]
                w = parts[0] if len(parts) == 1 else jnp.concatenate(parts, axis=0)
                acc[:n_tok] += dot(jnp.concatenate([t[...] for t in tok_a], axis=1), w)
                acc[n_tok:] += dot(jnp.concatenate([t[...] for t in tok_b], axis=1), w)

        if final:

            @pl.when(i == steps - 1)
            def _():
                outs[0][...] = acc[:n_tok].astype(BF)
                outs[1][...] = acc[n_tok:].astype(BF)

    tok_specs = [pl.BlockSpec((n_tok, blk), lambda i, s, k=k: (0, s[i * per + k])) for k in range(per)]
    shape = (2 * n_tok, n)
    return pl.pallas_call(
        body,
        out_shape=(jax.ShapeDtypeStruct((n_tok, n), BF),) * 2 if final else jax.ShapeDtypeStruct(shape, F32),
        grid_spec=pltpu.PrefetchScalarGridSpec(
            num_scalar_prefetch=1,
            grid=(steps,),
            in_specs=tok_specs * 2 + [once(w.shape) for w in flat] + extra_specs,
            out_specs=(whole((n_tok, n)),) * 2 if final else whole(shape),
            scratch_shapes=[pltpu.VMEM(shape, F32)] if final else [],
        ),
        compiler_params=pltpu.CompilerParams(vmem_limit_bytes=22 * MIB),
        cost_estimate=pl.CostEstimate(
            flops=20 * n_tok * rows * n * steps, bytes_accessed=8 * n_tok * rows * steps, transcendentals=0
        ),
    )(where_from, *([own] * per), *([other] * per), *flat, *extra)


def per_device(tokens, weight, down, up, cotangent, tasks, owned, counts):
    n_tok, width = tokens.shape
    kv = weight.shape[1]
    adapters = owned.shape[0]
    cols = adapters * RANK
    ny, nx, nz = lax.axis_size("y"), lax.axis_size("x"), lax.axis_size("z")
    me_c = lax.axis_index("c")
    d_rows, v_rows = width // (nx * nz * 2), kv // (nx * nz * 2)
    me_x, me_z = lax.axis_index("x"), lax.axis_index("z")
    sc = SLOTS * RANK
    lanes = nx * (d_rows + v_rows)
    half = kv // 2

    def columns(a, core):
        return lax.dynamic_slice_in_dim(a, core * half, half, 1)

    block_a = columns(weight, me_c)
    block_b = lax.ppermute(columns(weight, 1 - me_c), "c", SWAP)
    partner_tasks = lax.ppermute(tasks, "c", SWAP)
    other = lax.ppermute(tokens, "c", SWAP)
    block_b, partner_tasks, cotangent, counts = lax.optimization_barrier((block_b, partner_tasks, cotangent, counts))
    first_hop = [shifted(block_a, "x", k) for k in range(1, nx)] + [shifted(block_b, "z", k) for k in range(1, nz)]
    def blocks_a(step):
        z = (me_z + step) % nz
        return [(((me_x - k) % nx) * nz + z) * 2 + me_c for k in range(nx)]

    def blocks_b(step):
        x = (me_x + step) % nx
        return [(x * nz + (me_z - k) % nz) * 2 + 1 - me_c for k in range(nz)]

    def at(*lists):
        return jnp.stack([i for one in lists for i in one]).astype(jnp.int32)

    ids = jnp.arange(adapters, dtype=jnp.int32)
    hit = tasks[:, None] == ids[None, :]
    present = jnp.any(hit | (partner_tasks[:, None] == ids[None, :]), axis=0)
    rank_of = jnp.sum((ids[None, :] < ids[:, None]) & present[None, :], axis=1)
    col_slot = jnp.arange(sc, dtype=jnp.int32) // RANK
    col_rank = jnp.arange(sc, dtype=jnp.int32) % RANK
    row = jnp.arange(cols, dtype=jnp.int32)

    token_count = jnp.sum(jnp.where(hit, counts.astype(F32)[None, :], 0.0), axis=1)
    token_weight = (SCALE / token_count)[:, None]
    v_out = jnp.arange(kv, dtype=jnp.int32)
    v_from = (
        (v_out // v_rows % nx) * (nz * 2 * v_rows)
        + (v_out // (v_rows * nx) % nz) * (2 * v_rows)
        + v_out // (v_rows * nx * nz) * v_rows
        + v_out % v_rows
    )

    owned_col = jnp.repeat(owned.astype(F32), RANK)[:, None]

    def local_terms(first):
        chosen = present[None, :] & (rank_of[None, :] == first + col_slot[:, None])
        col_task = jnp.sum(jnp.where(chosen, ids[None, :] + 1, 0), axis=1) - 1
        more = (jnp.sum(present.astype(jnp.int32)) > first + SLOTS).astype(F32)
        pick_t = ((row // RANK)[None, :] == col_task[:, None]) & ((row % RANK)[None, :] == col_rank[:, None])
        pick_t = pick_t.astype(BF)
        hidden, theirs, mine = terms(
            tokens,
            down,
            up,
            cotangent,
            tasks,
            token_weight,
            pick_t,
            col_task,
            v_from,
            me_c.astype(jnp.int32)[None],
            nx,
            nz,
        )
        note_row = lax.broadcasted_iota(jnp.int32, (INFO, lanes), 0)
        note = jnp.where(note_row == 0, jnp.pad(col_task.astype(F32), (0, lanes - sc))[None, :], more)
        return hidden, theirs, mine, note.astype(BF)

    hidden, theirs, mine, note = local_terms(jnp.int32(0))
    first_hop, theirs, other = lax.optimization_barrier((first_hop, theirs, other))
    near_a, near_b = join([block_a] + first_hop[: nx - 1], [block_b] + first_hop[nx - 1 :])
    near_a, near_b, theirs, other = lax.optimization_barrier((near_a, near_b, theirs, other))
    got = lax.ppermute(theirs, "c", SWAP)
    a_down, a_up = shifted(near_a, "z", 1), shifted(near_a, "z", nz - 1)
    b_down, b_up = shifted(near_b, "x", 1), shifted(near_b, "x", nx - 1)
    pass_on = halves([a_down, a_up, b_down, b_up], [0, 1, 0, 1])
    a_far = [shifted(pass_on[0], "z", 1), shifted(pass_on[1], "z", nz - 1)]
    b_far = [shifted(pass_on[2], "x", 1), shifted(pass_on[3], "x", nx - 1)]

    from_z = exchange(pack(mine, got, note), "z")

    sent_hidden, _ = lax.optimization_barrier((hidden, got))
    other_hidden = lax.ppermute(sent_hidden, "c", SWAP)
    acc = add_blocks(
        tokens,
        other,
        [[near_a], [near_b]],
        at(blocks_a(0), blocks_b(0), [me_c]),
        lora=(hidden, other_hidden, up),
    )
    from_z, acc = lax.optimization_barrier((from_z, acc))
    from_y = exchange(spread(from_z, owned_col, ny), "y")
    by_x = turn(from_y, nx, d_rows)
    by_x, acc = lax.optimization_barrier((by_x, acc))
    grad_down, grad_up, flags = finish(exchange(by_x, "x"), d_rows)
    acc = add_blocks(
        tokens,
        other,
        [[a_down], [a_up], [b_down], [b_up]],
        at(blocks_a(-1), blocks_a(1), blocks_b(-1), blocks_b(1)),
        before=acc,
    )
    acc, flags = lax.optimization_barrier((acc, flags))
    tile, sent = add_blocks(tokens, other, [a_far, b_far], at(blocks_a(2), blocks_b(2)), before=acc, final=True)
    back = lax.ppermute(sent, "c", SWAP)
    keys = jnp.concatenate([jnp.where(me_c == 0, tile, back), jnp.where(me_c == 0, back, tile)], axis=1)

    flag, keys = lax.optimization_barrier((flags[0, 0], keys))

    def again(state):
        first, down_sum, up_sum, _ = state
        _, theirs, mine, note = local_terms(first)
        by_owner = spread(exchange(pack(mine, lax.ppermute(theirs, "c", SWAP), note), "z"), owned_col, ny)
        by_x = turn(exchange(by_owner, "y"), nx, d_rows)
        down_more, up_more, flags = finish(exchange(by_x, "x"), d_rows)
        return first + SLOTS, down_sum + down_more, up_sum + up_more, flags[0, 0]

    _, grad_down, grad_up, _ = lax.while_loop(
        lambda state: state[3] > 0.5, again, (jnp.int32(SLOTS), grad_down, grad_up, flag)
    )
    return keys, grad_down[None], grad_up[None]


def solution(mesh):
    sizes = dict(mesh.shape)
    ny = sizes["grp"]
    nx = nz = int((sizes["fsdp"] // 2) ** 0.5)
    fine = Mesh(mesh.devices.reshape(ny, nx, nz, 2), ("y", "x", "z", "c"))
    fsdp = ("x", "z", "c")
    every = ("y", "x", "z", "c")
    in_specs = (P(every, None), P(fsdp, None), P(), P(), P(every, None), P(every), P(), P())
    out_specs = (P(every, None), P("y", fsdp, None), P("y", fsdp, None))
    return jax.shard_map(per_device, mesh=fine, in_specs=in_specs, out_specs=out_specs, check_vma=False)
```

```python
import jax
import jax.numpy as jnp
from jax import lax
from jax.experimental import pallas as pl
from jax.experimental.pallas import tpu as pltpu
from jax.sharding import Mesh, PartitionSpec as P

RANK = 64
SCALE = 0.5
BF = jnp.bfloat16
F32 = jnp.float32
SLOTS = 2
INFO = 16
MIB = 1 << 20
SWAP = [(0, 1), (1, 0)]


def dot(a, b, dims=((1,), (0,))):
    return lax.dot_general(a, b, (dims, ((), ())), preferred_element_type=F32)


def exchange(a, axis):
    return lax.all_to_all(a, axis, 0, 0, tiled=True)


def call(body, out, grid, in_specs, out_specs, scratch=(), flops=0, data=0, vmem=12):
    return pl.pallas_call(
        body,
        out_shape=out,
        grid=grid,
        in_specs=in_specs,
        out_specs=out_specs,
        scratch_shapes=list(scratch),
        compiler_params=pltpu.CompilerParams(vmem_limit_bytes=vmem * MIB),
        cost_estimate=pl.CostEstimate(flops=flops, bytes_accessed=data, transcendentals=0),
    )


def whole(shape):
    return pl.BlockSpec(shape, lambda *i: (0,) * len(shape))


def once(shape):
    return pl.BlockSpec(shape, lambda *i: (0,) * len(shape), pipeline_mode=pl.Buffered(1))


def terms(tokens, down, up, cotangent, tasks, token_weight, pick_t, col_task, v_from, me_c, nx, nz):
    n_tok, width = tokens.shape
    cols = down.shape[1]
    sc = pick_t.shape[0]
    kv = cotangent.shape[1]
    per = 4
    steps = nx * nz // per
    blk = width // steps
    d = width // (nx * nz * 2)
    half = kv // 2
    u = half // nz
    lanes = nx * d + u

    def body(me, tok, dn, up_ref, cot, task_col, task_row, tw, pick, picked, v_ref, hidden, theirs, mine, acc, sca, low):
        i = pl.program_id(0)
        first = me[0] == 0

        @pl.when(i == 0)
        def _():
            sca[...] = (cot[...].astype(F32) * tw[...]).astype(BF)
            up_slot = dot(pick[...], up_ref[...], ((1,), (1,))).astype(BF)
            g = dot(up_slot, sca[...], ((1,), (1,)))
            low[...] = jnp.where(picked[...] == task_row[...], g, 0.0).astype(BF)

        t = tok[...]
        part = dot(t, dn[...])

        @pl.when(i == 0)
        def _():
            acc[...] = part

        @pl.when(i > 0)
        def _():
            acc[...] += part

        r = dot(low[...], t).astype(BF)
        for k in range(per):
            x, z = (i * per + k) // nz, (i * per + k) % nz
            at = pl.ds(pl.multiple_of(x * d, d), d)
            a, b = r[:, 2 * k * d : (2 * k + 1) * d], r[:, (2 * k + 1) * d : (2 * k + 2) * d]
            mine[z, :, at] = jnp.where(first, a, b)
            theirs[z, :, at] = jnp.where(first, b, a)

        @pl.when(i == steps - 1)
        def _():
            adapter = lax.broadcasted_iota(jnp.int32, (n_tok, cols), 1) // RANK
            h = jnp.where(task_col[...] == adapter, acc[...], 0.0).astype(BF)
            hidden[...] = h
            h_t = dot(pick[...], h, ((1,), (1,))).astype(BF)
            order = lax.broadcasted_iota(jnp.int32, (kv, kv), 0) == v_ref[...]
            g = dot(dot(h_t, sca[...]).astype(BF), jnp.where(order, 1.0, 0.0).astype(BF)).astype(BF)
            for k in range(nz):
                a, b = g[:, k * u : (k + 1) * u], g[:, half + k * u : half + (k + 1) * u]
                mine[k, :, nx * d :] = jnp.where(first, a, b)
                theirs[k, :, nx * d :] = jnp.where(first, b, a)

    return call(
        body,
        (
            jax.ShapeDtypeStruct((n_tok, cols), BF),
            jax.ShapeDtypeStruct((nz, sc, lanes), BF),
            jax.ShapeDtypeStruct((nz, sc, lanes), BF),
        ),
        (steps,),
        [
            pl.BlockSpec(memory_space=pltpu.SMEM),
            pl.BlockSpec((n_tok, blk), lambda i: (0, i)),
            pl.BlockSpec((blk, cols), lambda i: (i, 0)),
            once((kv, cols)),
            once((n_tok, kv)),
            once((n_tok, 1)),
            once((1, n_tok)),
            once((n_tok, 1)),
            once((sc, cols)),
            once((sc, 1)),
            once((1, kv)),
        ],
        (whole((n_tok, cols)), whole((nz, sc, lanes)), whole((nz, sc, lanes))),
        [pltpu.VMEM((n_tok, cols), F32), pltpu.VMEM((n_tok, kv), BF), pltpu.VMEM((sc, n_tok), BF)],
        flops=2 * n_tok * width * (cols + sc),
        data=24 * MIB,
        vmem=28,
    )(
        me_c,
        tokens,
        down,
        up,
        cotangent,
        tasks[:, None],
        tasks[None, :],
        token_weight,
        pick_t,
        col_task[:, None],
        v_from[None, :],
    )


def join(*lists):
    n = len(lists[0])
    rows, lanes = lists[0][0].shape

    def body(*refs):
        for k in range(len(lists)):
            for j in range(n):
                refs[n * len(lists) + k][j * rows : (j + 1) * rows] = refs[k * n + j][...]

    return call(
        body,
        tuple(jax.ShapeDtypeStruct((n * rows, lanes), BF) for _ in lists),
        (1,),
        [once((rows, lanes))] * (n * len(lists)),
        tuple(whole((n * rows, lanes)) for _ in lists),
        data=4 * MIB,
    )(*[a for one in lists for a in one])


def halves(arrays, which):
    rows, lanes = arrays[0].shape
    steps = 2
    blk = rows // 2 // steps

    def body(*refs):
        for k in range(len(arrays)):
            refs[len(arrays) + k][...] = refs[k][...]

    return call(
        body,
        tuple(jax.ShapeDtypeStruct((rows // 2, lanes), BF) for _ in arrays),
        (steps,),
        [pl.BlockSpec((blk, lanes), lambda i, w=w: (w * steps + i, 0)) for w in which],
        tuple(pl.BlockSpec((blk, lanes), lambda i: (i, 0)) for _ in arrays),
        data=4 * MIB,
    )(*arrays)


def pack(mine, theirs, note):
    n, sc, lanes = mine.shape

    def body(a, b, c, out):
        out[0, :sc] = (a[0].astype(F32) + b[0].astype(F32)).astype(BF)
        out[0, sc:] = c[...]

    block = pl.BlockSpec((1, sc, lanes), lambda i: (i, 0, 0))
    return call(
        body,
        jax.ShapeDtypeStruct((n, sc + INFO, lanes), BF),
        (n,),
        [block, block, whole((INFO, lanes))],
        pl.BlockSpec((1, sc + INFO, lanes), lambda i: (i, 0, 0)),
        data=10 * MIB,
    )(mine, theirs, note)


def spread(got, owned_col, ny):
    n, rows, lanes = got.shape
    sc = rows - INFO
    cols = owned_col.shape[0]
    own = cols // ny

    def body(g, ow, out):
        total = jnp.zeros((own, lanes), F32)
        flag = jnp.zeros((1, lanes), BF)
        same = (
            lax.broadcasted_iota(jnp.int32, (own, sc), 0) % RANK
            == lax.broadcasted_iota(jnp.int32, (own, sc), 1) % RANK
        )
        for p in range(n):
            note = g[p, sc:, :]
            sent = note[0:1, :sc].astype(F32)
            place = jnp.where(same & (ow[...] == sent), 1.0, 0.0).astype(BF)
            total += dot(place, g[p, :sc, :])
            flag = jnp.maximum(flag, note[1:2, :])
        out[0, :own] = total.astype(BF)
        out[0, own:] = jnp.broadcast_to(flag, (INFO, lanes))

    return call(
        body,
        jax.ShapeDtypeStruct((ny, own + INFO, lanes), BF),
        (ny,),
        [once((n, rows, lanes)), pl.BlockSpec((own, 1), lambda i: (i, 0))],
        pl.BlockSpec((1, own + INFO, lanes), lambda i: (i, 0, 0)),
        flops=2 * cols * n * sc * lanes,
        data=5 * MIB,
    )(got, owned_col)


def turn(got, nx, d):
    n, rows, lanes = got.shape
    own = rows - INFO
    v = (lanes - nx * d) // nx

    def body(g, out):
        total = g[0, :own].astype(F32)
        flag = g[0, own : own + INFO, :own]
        for p in range(1, n):
            total += g[p, :own].astype(F32)
            flag = jnp.maximum(flag, g[p, own : own + INFO, :own])
        t = total.T.astype(BF)
        for x in range(nx):
            out[x, :d] = t[x * d : (x + 1) * d]
            out[x, d : d + v] = t[nx * d + x * v : nx * d + (x + 1) * v]
            out[x, d + v :] = flag

    return call(
        body,
        jax.ShapeDtypeStruct((nx, d + v + INFO, own), BF),
        (1,),
        [whole(got.shape)],
        whole((nx, d + v + INFO, own)),
        data=2 * MIB,
    )(got)


def finish(got, d):
    n, rows, own = got.shape
    v = rows - INFO - d

    def body(g, down, up, flag):
        total = g[0].astype(F32)
        most = g[0, d + v :].astype(F32)
        for p in range(1, n):
            total += g[p].astype(F32)
            most = jnp.maximum(most, g[p, d + v :].astype(F32))
        down[...] = total[:d]
        up[...] = total[d : d + v]
        flag[...] = most

    shapes = (d, own), (v, own), (INFO, own)
    return call(
        body,
        tuple(jax.ShapeDtypeStruct(s, F32) for s in shapes),
        (1,),
        [whole(got.shape)],
        tuple(whole(s) for s in shapes),
        data=MIB // 2,
    )(got)


def shifted(a, axis, step):
    n = lax.axis_size(axis)
    return lax.ppermute(a, axis, [(i, (i + step) % n) for i in range(n)])


def add_blocks(own, other, groups, where_from, before=None, lora=None, final=False):
    n_tok = own.shape[0]
    rows = sum(w.shape[0] for w in groups[0])
    n = groups[0][0].shape[1]
    steps = len(groups)
    per = where_from.shape[0] // steps
    blk = rows // per
    flat = [w for group in groups for w in group]
    extra = [] if before is None else [before]
    extra_specs = [once(e.shape) for e in extra]
    if lora is not None:
        extra += list(lora)
        extra_specs += [once(e.shape) for e in lora[:2]]
        extra_specs.append(pl.BlockSpec((n, lora[2].shape[1]), lambda i, s: (s[steps * per], 0)))

    def body(at, *refs):
        tok_a, tok_b = refs[:per], refs[per : 2 * per]
        ws = refs[2 * per : 2 * per + len(flat)]
        more = refs[2 * per + len(flat) : 2 * per + len(flat) + len(extra)]
        outs = refs[2 * per + len(flat) + len(extra) :]
        acc = refs[-1]
        i = pl.program_id(0)

        @pl.when(i == 0)
        def _():
            if before is not None:
                acc[...] = more[0][...]
            else:
                acc[...] = jnp.zeros_like(acc)
            if lora is not None:
                h_a, h_b, u = more[-3:]
                acc[:n_tok] += SCALE * dot(h_a[...], u[...], ((1,), (1,)))
                acc[n_tok:] += SCALE * dot(h_b[...], u[...], ((1,), (1,)))

        left = 0
        for p in range(steps):
            mine = ws[left : left + len(groups[p])]
            left += len(groups[p])

            @pl.when(i == p)
            def _(mine=mine):
                parts = [w[...] for w in mine]
                w = parts[0] if len(parts) == 1 else jnp.concatenate(parts, axis=0)
                acc[:n_tok] += dot(jnp.concatenate([t[...] for t in tok_a], axis=1), w)
                acc[n_tok:] += dot(jnp.concatenate([t[...] for t in tok_b], axis=1), w)

        if final:

            @pl.when(i == steps - 1)
            def _():
                outs[0][...] = acc[:n_tok].astype(BF)
                outs[1][...] = acc[n_tok:].astype(BF)

    tok_specs = [pl.BlockSpec((n_tok, blk), lambda i, s, k=k: (0, s[i * per + k])) for k in range(per)]
    shape = (2 * n_tok, n)
    return pl.pallas_call(
        body,
        out_shape=(jax.ShapeDtypeStruct((n_tok, n), BF),) * 2 if final else jax.ShapeDtypeStruct(shape, F32),
        grid_spec=pltpu.PrefetchScalarGridSpec(
            num_scalar_prefetch=1,
            grid=(steps,),
            in_specs=tok_specs * 2 + [once(w.shape) for w in flat] + extra_specs,
            out_specs=(whole((n_tok, n)),) * 2 if final else whole(shape),
            scratch_shapes=[pltpu.VMEM(shape, F32)] if final else [],
        ),
        compiler_params=pltpu.CompilerParams(vmem_limit_bytes=22 * MIB),
        cost_estimate=pl.CostEstimate(
            flops=4 * n_tok * rows * n * steps, bytes_accessed=8 * n_tok * rows * steps, transcendentals=0
        ),
    )(where_from, *([own] * per), *([other] * per), *flat, *extra)


def per_device(tokens, weight, down, up, cotangent, tasks, owned, counts):
    n_tok, width = tokens.shape
    kv = weight.shape[1]
    adapters = owned.shape[0]
    cols = adapters * RANK
    ny, nx, nz = lax.axis_size("y"), lax.axis_size("x"), lax.axis_size("z")
    me_c = lax.axis_index("c")
    d_rows, v_rows = width // (nx * nz * 2), kv // (nx * nz * 2)
    me_x, me_z = lax.axis_index("x"), lax.axis_index("z")
    sc = SLOTS * RANK
    lanes = nx * (d_rows + v_rows)
    half = kv // 2

    def columns(a, core):
        return lax.dynamic_slice_in_dim(a, core * half, half, 1)

    block_a = columns(weight, me_c)
    block_b = lax.ppermute(columns(weight, 1 - me_c), "c", SWAP)
    partner_tasks = lax.ppermute(tasks, "c", SWAP)
    block_b, partner_tasks, cotangent, counts = lax.optimization_barrier((block_b, partner_tasks, cotangent, counts))
    first_hop = [shifted(block_a, "x", k) for k in range(1, nx)] + [shifted(block_b, "z", k) for k in range(1, nz)]
    def blocks_a(step):
        z = (me_z + step) % nz
        return [(((me_x - k) % nx) * nz + z) * 2 + me_c for k in range(nx)]

    def blocks_b(step):
        x = (me_x + step) % nx
        return [(x * nz + (me_z - k) % nz) * 2 + 1 - me_c for k in range(nz)]

    def at(*lists):
        return jnp.stack([i for one in lists for i in one]).astype(jnp.int32)

    ids = jnp.arange(adapters, dtype=jnp.int32)
    hit = tasks[:, None] == ids[None, :]
    present = jnp.any(hit | (partner_tasks[:, None] == ids[None, :]), axis=0)
    rank_of = jnp.sum((ids[None, :] < ids[:, None]) & present[None, :], axis=1)
    col_slot = jnp.arange(sc, dtype=jnp.int32) // RANK
    col_rank = jnp.arange(sc, dtype=jnp.int32) % RANK
    row = jnp.arange(cols, dtype=jnp.int32)

    token_count = jnp.sum(jnp.where(hit, counts.astype(F32)[None, :], 0.0), axis=1)
    token_weight = (SCALE / token_count)[:, None]
    v_out = jnp.arange(kv, dtype=jnp.int32)
    v_from = (
        (v_out // v_rows % nx) * (nz * 2 * v_rows)
        + (v_out // (v_rows * nx) % nz) * (2 * v_rows)
        + v_out // (v_rows * nx * nz) * v_rows
        + v_out % v_rows
    )

    owned_col = jnp.repeat(owned.astype(F32), RANK)[:, None]

    def local_terms(first):
        chosen = present[None, :] & (rank_of[None, :] == first + col_slot[:, None])
        col_task = jnp.sum(jnp.where(chosen, ids[None, :] + 1, 0), axis=1) - 1
        more = (jnp.sum(present.astype(jnp.int32)) > first + SLOTS).astype(F32)
        pick_t = ((row // RANK)[None, :] == col_task[:, None]) & ((row % RANK)[None, :] == col_rank[:, None])
        pick_t = pick_t.astype(BF)
        hidden, theirs, mine = terms(
            tokens,
            down,
            up,
            cotangent,
            tasks,
            token_weight,
            pick_t,
            col_task,
            v_from,
            me_c.astype(jnp.int32)[None],
            nx,
            nz,
        )
        note_row = lax.broadcasted_iota(jnp.int32, (INFO, lanes), 0)
        note = jnp.where(note_row == 0, jnp.pad(col_task.astype(F32), (0, lanes - sc))[None, :], more)
        return hidden, theirs, mine, note.astype(BF)

    hidden, theirs, mine, note = local_terms(jnp.int32(0))
    first_hop, theirs = lax.optimization_barrier((first_hop, theirs))
    near_a, near_b = join([block_a] + first_hop[: nx - 1], [block_b] + first_hop[nx - 1 :])
    near_a, near_b, theirs, sent_hidden = lax.optimization_barrier((near_a, near_b, theirs, hidden))
    got = lax.ppermute(theirs, "c", SWAP)
    other_hidden = lax.ppermute(sent_hidden, "c", SWAP)
    chip = pack(mine, got, note)
    sent_tokens, _ = lax.optimization_barrier((tokens, got))
    other = lax.ppermute(sent_tokens, "c", SWAP)
    near_a, other, _ = lax.optimization_barrier((near_a, other, chip))
    a_down, a_up = shifted(near_a, "z", 1), shifted(near_a, "z", nz - 1)
    b_down, b_up = shifted(near_b, "x", 1), shifted(near_b, "x", nx - 1)
    from_z = exchange(chip, "z")

    acc = add_blocks(
        tokens,
        other,
        [[near_a], [near_b]],
        at(blocks_a(0), blocks_b(0), [me_c]),
        lora=(hidden, other_hidden, up),
    )
    from_z, acc = lax.optimization_barrier((from_z, acc))
    b_down, b_up, _ = lax.optimization_barrier((b_down, b_up, from_z))
    from_y = exchange(spread(from_z, owned_col, ny), "y")
    b_pass = halves([b_down, b_up], [0, 1])
    b_far = [shifted(b_pass[0], "x", 1), shifted(b_pass[1], "x", nx - 1)]
    acc = add_blocks(tokens, other, [[b_down], [b_up]], at(blocks_b(-1), blocks_b(1)), before=acc)
    a_down, a_up, acc = lax.optimization_barrier((a_down, a_up, acc))
    a_pass = halves([a_down, a_up], [0, 1])
    a_far = [shifted(a_pass[0], "z", 1), shifted(a_pass[1], "z", nz - 1)]
    by_x = turn(from_y, nx, d_rows)
    by_x, acc = lax.optimization_barrier((by_x, acc))
    from_x = exchange(by_x, "x")
    acc = add_blocks(tokens, other, [[a_down], [a_up]], at(blocks_a(-1), blocks_a(1)), before=acc)
    acc, from_x = lax.optimization_barrier((acc, from_x))
    tile, sent = add_blocks(tokens, other, [a_far, b_far], at(blocks_a(2), blocks_b(2)), before=acc, final=True)
    grad_down, grad_up, flags = finish(from_x, d_rows)
    back = lax.ppermute(sent, "c", SWAP)
    keys = jnp.concatenate([jnp.where(me_c == 0, tile, back), jnp.where(me_c == 0, back, tile)], axis=1)

    flag, keys = lax.optimization_barrier((flags[0, 0], keys))

    def again(state):
        first, down_sum, up_sum, _ = state
        _, theirs, mine, note = local_terms(first)
        by_owner = spread(exchange(pack(mine, lax.ppermute(theirs, "c", SWAP), note), "z"), owned_col, ny)
        by_x = turn(exchange(by_owner, "y"), nx, d_rows)
        down_more, up_more, flags = finish(exchange(by_x, "x"), d_rows)
        return first + SLOTS, down_sum + down_more, up_sum + up_more, flags[0, 0]

    _, grad_down, grad_up, _ = lax.while_loop(
        lambda state: state[3] > 0.5, again, (jnp.int32(SLOTS), grad_down, grad_up, flag)
    )
    return keys, grad_down[None], grad_up[None]


def solution(mesh):
    sizes = dict(mesh.shape)
    ny = sizes["grp"]
    nx = nz = int((sizes["fsdp"] // 2) ** 0.5)
    fine = Mesh(mesh.devices.reshape(ny, nx, nz, 2), ("y", "x", "z", "c"))
    fsdp = ("x", "z", "c")
    every = ("y", "x", "z", "c")
    in_specs = (P(every, None), P(fsdp, None), P(), P(), P(every, None), P(every), P(), P())
    out_specs = (P(every, None), P("y", fsdp, None), P("y", fsdp, None))
    return jax.shard_map(per_device, mesh=fine, in_specs=in_specs, out_specs=out_specs, check_vma=False)
```

```python
import jax
import jax.numpy as jnp
from jax import lax
from jax.experimental import pallas as pl
from jax.experimental.pallas import tpu as pltpu
from jax.sharding import Mesh, PartitionSpec as P

RANK = 64
SCALE = 0.5
BF = jnp.bfloat16
F32 = jnp.float32
SLOTS = 2
INFO = 16
MIB = 1 << 20
SWAP = [(0, 1), (1, 0)]


def dot(a, b, dims=((1,), (0,))):
    return lax.dot_general(a, b, (dims, ((), ())), preferred_element_type=F32)


def exchange(a, axis):
    return lax.all_to_all(a, axis, 0, 0, tiled=True)


def call(body, out, grid, in_specs, out_specs, scratch=(), flops=0, data=0, vmem=12):
    return pl.pallas_call(
        body,
        out_shape=out,
        grid=grid,
        in_specs=in_specs,
        out_specs=out_specs,
        scratch_shapes=list(scratch),
        compiler_params=pltpu.CompilerParams(vmem_limit_bytes=vmem * MIB),
        cost_estimate=pl.CostEstimate(flops=flops, bytes_accessed=data, transcendentals=0),
    )


def whole(shape):
    return pl.BlockSpec(shape, lambda *i: (0,) * len(shape))


def once(shape):
    return pl.BlockSpec(shape, lambda *i: (0,) * len(shape), pipeline_mode=pl.Buffered(1))


def terms(tokens, down, up, cotangent, tasks, token_weight, pick_t, col_task, v_from, me_c, nx, nz):
    n_tok, width = tokens.shape
    cols = down.shape[1]
    sc = pick_t.shape[0]
    kv = cotangent.shape[1]
    per = 4
    steps = nx * nz // per
    blk = width // steps
    d = width // (nx * nz * 2)
    half = kv // 2
    u = half // nz
    lanes = nx * d + u

    def body(me, tok, dn, up_ref, cot, task_col, task_row, tw, pick, picked, v_ref, hidden, theirs, mine, acc, sca, low):
        i = pl.program_id(0)
        first = me[0] == 0

        @pl.when(i == 0)
        def _():
            sca[...] = (cot[...].astype(F32) * tw[...]).astype(BF)
            up_slot = dot(pick[...], up_ref[...], ((1,), (1,))).astype(BF)
            g = dot(up_slot, sca[...], ((1,), (1,)))
            low[...] = jnp.where(picked[...] == task_row[...], g, 0.0).astype(BF)

        t = tok[...]
        part = dot(t, dn[...])

        @pl.when(i == 0)
        def _():
            acc[...] = part

        @pl.when(i > 0)
        def _():
            acc[...] += part

        r = dot(low[...], t).astype(BF)
        for k in range(per):
            x, z = (i * per + k) // nz, (i * per + k) % nz
            at = pl.ds(pl.multiple_of(x * d, d), d)
            a, b = r[:, 2 * k * d : (2 * k + 1) * d], r[:, (2 * k + 1) * d : (2 * k + 2) * d]
            mine[z, :, at] = jnp.where(first, a, b)
            theirs[z, :, at] = jnp.where(first, b, a)

        @pl.when(i == steps - 1)
        def _():
            adapter = lax.broadcasted_iota(jnp.int32, (n_tok, cols), 1) // RANK
            h = jnp.where(task_col[...] == adapter, acc[...], 0.0).astype(BF)
            hidden[...] = h
            h_t = dot(pick[...], h, ((1,), (1,))).astype(BF)
            order = lax.broadcasted_iota(jnp.int32, (kv, kv), 0) == v_ref[...]
            g = dot(dot(h_t, sca[...]).astype(BF), jnp.where(order, 1.0, 0.0).astype(BF)).astype(BF)
            for k in range(nz):
                a, b = g[:, k * u : (k + 1) * u], g[:, half + k * u : half + (k + 1) * u]
                mine[k, :, nx * d :] = jnp.where(first, a, b)
                theirs[k, :, nx * d :] = jnp.where(first, b, a)

    return call(
        body,
        (
            jax.ShapeDtypeStruct((n_tok, cols), BF),
            jax.ShapeDtypeStruct((nz, sc, lanes), BF),
            jax.ShapeDtypeStruct((nz, sc, lanes), BF),
        ),
        (steps,),
        [
            pl.BlockSpec(memory_space=pltpu.SMEM),
            pl.BlockSpec((n_tok, blk), lambda i: (0, i)),
            pl.BlockSpec((blk, cols), lambda i: (i, 0)),
            once((kv, cols)),
            once((n_tok, kv)),
            once((n_tok, 1)),
            once((1, n_tok)),
            once((n_tok, 1)),
            once((sc, cols)),
            once((sc, 1)),
            once((1, kv)),
        ],
        (whole((n_tok, cols)), whole((nz, sc, lanes)), whole((nz, sc, lanes))),
        [pltpu.VMEM((n_tok, cols), F32), pltpu.VMEM((n_tok, kv), BF), pltpu.VMEM((sc, n_tok), BF)],
        flops=2 * n_tok * width * (cols + sc),
        data=24 * MIB,
        vmem=28,
    )(
        me_c,
        tokens,
        down,
        up,
        cotangent,
        tasks[:, None],
        tasks[None, :],
        token_weight,
        pick_t,
        col_task[:, None],
        v_from[None, :],
    )


def join(*lists):
    n = len(lists[0])
    rows, lanes = lists[0][0].shape

    def body(*refs):
        for k in range(len(lists)):
            for j in range(n):
                refs[n * len(lists) + k][j * rows : (j + 1) * rows] = refs[k * n + j][...]

    return call(
        body,
        tuple(jax.ShapeDtypeStruct((n * rows, lanes), BF) for _ in lists),
        (1,),
        [once((rows, lanes))] * (n * len(lists)),
        tuple(whole((n * rows, lanes)) for _ in lists),
        data=4 * MIB,
    )(*[a for one in lists for a in one])


def halves(arrays, which):
    rows, lanes = arrays[0].shape
    steps = 2
    blk = rows // 2 // steps

    def body(*refs):
        for k in range(len(arrays)):
            refs[len(arrays) + k][...] = refs[k][...]

    return call(
        body,
        tuple(jax.ShapeDtypeStruct((rows // 2, lanes), BF) for _ in arrays),
        (steps,),
        [pl.BlockSpec((blk, lanes), lambda i, w=w: (w * steps + i, 0)) for w in which],
        tuple(pl.BlockSpec((blk, lanes), lambda i: (i, 0)) for _ in arrays),
        data=4 * MIB,
    )(*arrays)


def pack(mine, theirs, note):
    n, sc, lanes = mine.shape

    def body(a, b, c, out):
        out[0, :sc] = (a[0].astype(F32) + b[0].astype(F32)).astype(BF)
        out[0, sc:] = c[...]

    block = pl.BlockSpec((1, sc, lanes), lambda i: (i, 0, 0))
    return call(
        body,
        jax.ShapeDtypeStruct((n, sc + INFO, lanes), BF),
        (n,),
        [block, block, whole((INFO, lanes))],
        pl.BlockSpec((1, sc + INFO, lanes), lambda i: (i, 0, 0)),
        data=10 * MIB,
    )(mine, theirs, note)


def spread(got, owned_col, ny):
    n, rows, lanes = got.shape
    sc = rows - INFO
    cols = owned_col.shape[0]
    own = cols // ny

    def body(g, ow, out):
        total = jnp.zeros((own, lanes), F32)
        flag = jnp.zeros((1, lanes), BF)
        same = (
            lax.broadcasted_iota(jnp.int32, (own, sc), 0) % RANK
            == lax.broadcasted_iota(jnp.int32, (own, sc), 1) % RANK
        )
        for p in range(n):
            note = g[p, sc:, :]
            sent = note[0:1, :sc].astype(F32)
            place = jnp.where(same & (ow[...] == sent), 1.0, 0.0).astype(BF)
            total += dot(place, g[p, :sc, :])
            flag = jnp.maximum(flag, note[1:2, :])
        out[0, :own] = total.astype(BF)
        out[0, own:] = jnp.broadcast_to(flag, (INFO, lanes))

    return call(
        body,
        pltpu.HBM((ny, own + INFO, lanes), BF),
        (ny,),
        [once((n, rows, lanes)), pl.BlockSpec((own, 1), lambda i: (i, 0))],
        pl.BlockSpec((1, own + INFO, lanes), lambda i: (i, 0, 0)),
        flops=2 * cols * n * sc * lanes,
        data=5 * MIB,
    )(got, owned_col)


def turn(got, nx, d):
    n, rows, lanes = got.shape
    own = rows - INFO
    v = (lanes - nx * d) // nx

    def body(g, out):
        total = g[0, :own].astype(F32)
        flag = g[0, own : own + INFO, :own]
        for p in range(1, n):
            total += g[p, :own].astype(F32)
            flag = jnp.maximum(flag, g[p, own : own + INFO, :own])
        t = total.T.astype(BF)
        for x in range(nx):
            out[x, :d] = t[x * d : (x + 1) * d]
            out[x, d : d + v] = t[nx * d + x * v : nx * d + (x + 1) * v]
            out[x, d + v :] = flag

    return call(
        body,
        pltpu.HBM((nx, d + v + INFO, own), BF),
        (1,),
        [whole(got.shape)],
        whole((nx, d + v + INFO, own)),
        data=2 * MIB,
    )(got)


def finish(got, d):
    n, rows, own = got.shape
    v = rows - INFO - d

    def body(g, down, up, flag):
        total = g[0].astype(F32)
        most = g[0, d + v :].astype(F32)
        for p in range(1, n):
            total += g[p].astype(F32)
            most = jnp.maximum(most, g[p, d + v :].astype(F32))
        down[...] = total[:d]
        up[...] = total[d : d + v]
        flag[...] = most

    shapes = (d, own), (v, own), (INFO, own)
    return call(
        body,
        tuple(jax.ShapeDtypeStruct(s, F32) for s in shapes),
        (1,),
        [whole(got.shape)],
        tuple(whole(s) for s in shapes),
        data=MIB // 2,
    )(got)


def shifted(a, axis, step):
    n = lax.axis_size(axis)
    return lax.ppermute(a, axis, [(i, (i + step) % n) for i in range(n)])


def add_blocks(own, other, groups, where_from, before=None, lora=None, final=False):
    n_tok = own.shape[0]
    rows = sum(w.shape[0] for w in groups[0])
    n = groups[0][0].shape[1]
    steps = len(groups)
    per = where_from.shape[0] // steps
    blk = rows // per
    flat = [w for group in groups for w in group]
    extra = [] if before is None else [before]
    extra_specs = [once(e.shape) for e in extra]
    if lora is not None:
        extra += list(lora)
        extra_specs += [once(e.shape) for e in lora[:2]]
        extra_specs.append(pl.BlockSpec((n, lora[2].shape[1]), lambda i, s: (s[steps * per], 0)))

    def body(at, *refs):
        tok_a, tok_b = refs[:per], refs[per : 2 * per]
        ws = refs[2 * per : 2 * per + len(flat)]
        more = refs[2 * per + len(flat) : 2 * per + len(flat) + len(extra)]
        outs = refs[2 * per + len(flat) + len(extra) :]
        acc = refs[-1]
        i = pl.program_id(0)

        @pl.when(i == 0)
        def _():
            if before is not None:
                acc[...] = more[0][...]
            else:
                acc[...] = jnp.zeros_like(acc)
            if lora is not None:
                h_a, h_b, u = more[-3:]
                acc[:n_tok] += SCALE * dot(h_a[...], u[...], ((1,), (1,)))
                acc[n_tok:] += SCALE * dot(h_b[...], u[...], ((1,), (1,)))

        left = 0
        for p in range(steps):
            mine = ws[left : left + len(groups[p])]
            left += len(groups[p])

            @pl.when(i == p)
            def _(mine=mine):
                parts = [w[...] for w in mine]
                w = parts[0] if len(parts) == 1 else jnp.concatenate(parts, axis=0)
                acc[:n_tok] += dot(jnp.concatenate([t[...] for t in tok_a], axis=1), w)
                acc[n_tok:] += dot(jnp.concatenate([t[...] for t in tok_b], axis=1), w)

        if final:

            @pl.when(i == steps - 1)
            def _():
                outs[0][...] = acc[:n_tok].astype(BF)
                outs[1][...] = acc[n_tok:].astype(BF)

    tok_specs = [pl.BlockSpec((n_tok, blk), lambda i, s, k=k: (0, s[i * per + k])) for k in range(per)]
    shape = (2 * n_tok, n)
    return pl.pallas_call(
        body,
        out_shape=(jax.ShapeDtypeStruct((n_tok, n), BF),) * 2 if final else pltpu.HBM(shape, F32),
        grid_spec=pltpu.PrefetchScalarGridSpec(
            num_scalar_prefetch=1,
            grid=(steps,),
            in_specs=tok_specs * 2 + [once(w.shape) for w in flat] + extra_specs,
            out_specs=(whole((n_tok, n)),) * 2 if final else whole(shape),
            scratch_shapes=[pltpu.VMEM(shape, F32)] if final else [],
        ),
        compiler_params=pltpu.CompilerParams(vmem_limit_bytes=22 * MIB),
        cost_estimate=pl.CostEstimate(
            flops=4 * n_tok * rows * n * steps, bytes_accessed=8 * n_tok * rows * steps, transcendentals=0
        ),
    )(where_from, *([own] * per), *([other] * per), *flat, *extra)


def per_device(tokens, weight, down, up, cotangent, tasks, owned, counts):
    n_tok, width = tokens.shape
    kv = weight.shape[1]
    adapters = owned.shape[0]
    cols = adapters * RANK
    ny, nx, nz = lax.axis_size("y"), lax.axis_size("x"), lax.axis_size("z")
    me_c = lax.axis_index("c")
    d_rows, v_rows = width // (nx * nz * 2), kv // (nx * nz * 2)
    me_x, me_z = lax.axis_index("x"), lax.axis_index("z")
    sc = SLOTS * RANK
    lanes = nx * (d_rows + v_rows)
    half = kv // 2

    def columns(a, core):
        return lax.dynamic_slice_in_dim(a, core * half, half, 1)

    block_a = columns(weight, me_c)
    block_b = lax.ppermute(columns(weight, 1 - me_c), "c", SWAP)
    partner_tasks = lax.ppermute(tasks, "c", SWAP)
    block_b, partner_tasks, cotangent, counts = lax.optimization_barrier((block_b, partner_tasks, cotangent, counts))
    first_hop = [shifted(block_a, "x", k) for k in range(1, nx)] + [shifted(block_b, "z", k) for k in range(1, nz)]
    def blocks_a(step):
        z = (me_z + step) % nz
        return [(((me_x - k) % nx) * nz + z) * 2 + me_c for k in range(nx)]

    def blocks_b(step):
        x = (me_x + step) % nx
        return [(x * nz + (me_z - k) % nz) * 2 + 1 - me_c for k in range(nz)]

    def at(*lists):
        return jnp.stack([i for one in lists for i in one]).astype(jnp.int32)

    ids = jnp.arange(adapters, dtype=jnp.int32)
    hit = tasks[:, None] == ids[None, :]
    present = jnp.any(hit | (partner_tasks[:, None] == ids[None, :]), axis=0)
    rank_of = jnp.sum((ids[None, :] < ids[:, None]) & present[None, :], axis=1)
    col_slot = jnp.arange(sc, dtype=jnp.int32) // RANK
    col_rank = jnp.arange(sc, dtype=jnp.int32) % RANK
    row = jnp.arange(cols, dtype=jnp.int32)

    token_count = jnp.sum(jnp.where(hit, counts.astype(F32)[None, :], 0.0), axis=1)
    token_weight = (SCALE / token_count)[:, None]
    v_out = jnp.arange(kv, dtype=jnp.int32)
    v_from = (
        (v_out // v_rows % nx) * (nz * 2 * v_rows)
        + (v_out // (v_rows * nx) % nz) * (2 * v_rows)
        + v_out // (v_rows * nx * nz) * v_rows
        + v_out % v_rows
    )

    owned_col = jnp.repeat(owned.astype(F32), RANK)[:, None]

    def local_terms(first):
        chosen = present[None, :] & (rank_of[None, :] == first + col_slot[:, None])
        col_task = jnp.sum(jnp.where(chosen, ids[None, :] + 1, 0), axis=1) - 1
        more = (jnp.sum(present.astype(jnp.int32)) > first + SLOTS).astype(F32)
        pick_t = ((row // RANK)[None, :] == col_task[:, None]) & ((row % RANK)[None, :] == col_rank[:, None])
        pick_t = pick_t.astype(BF)
        hidden, theirs, mine = terms(
            tokens,
            down,
            up,
            cotangent,
            tasks,
            token_weight,
            pick_t,
            col_task,
            v_from,
            me_c.astype(jnp.int32)[None],
            nx,
            nz,
        )
        note_row = lax.broadcasted_iota(jnp.int32, (INFO, lanes), 0)
        note = jnp.where(note_row == 0, jnp.pad(col_task.astype(F32), (0, lanes - sc))[None, :], more)
        return hidden, theirs, mine, note.astype(BF)

    hidden, theirs, mine, note = local_terms(jnp.int32(0))
    first_hop, theirs = lax.optimization_barrier((first_hop, theirs))
    near_a, near_b = join([block_a] + first_hop[: nx - 1], [block_b] + first_hop[nx - 1 :])
    near_a, near_b, theirs, sent_hidden = lax.optimization_barrier((near_a, near_b, theirs, hidden))
    got = lax.ppermute(theirs, "c", SWAP)
    other_hidden = lax.ppermute(sent_hidden, "c", SWAP)
    chip = pack(mine, got, note)
    sent_tokens, _ = lax.optimization_barrier((tokens, got))
    other = lax.ppermute(sent_tokens, "c", SWAP)
    near_a, other, _ = lax.optimization_barrier((near_a, other, chip))
    a_down, a_up = shifted(near_a, "z", 1), shifted(near_a, "z", nz - 1)
    b_down, b_up = shifted(near_b, "x", 1), shifted(near_b, "x", nx - 1)
    from_z = exchange(chip, "z")

    acc = add_blocks(
        tokens,
        other,
        [[near_a], [near_b]],
        at(blocks_a(0), blocks_b(0), [me_c]),
        lora=(hidden, other_hidden, up),
    )
    from_z, acc = lax.optimization_barrier((from_z, acc))
    b_down, b_up, _ = lax.optimization_barrier((b_down, b_up, from_z))
    from_y = exchange(spread(from_z, owned_col, ny), "y")
    b_pass = halves([b_down, b_up], [0, 1])
    b_far = [shifted(b_pass[0], "x", 1), shifted(b_pass[1], "x", nx - 1)]
    acc = add_blocks(tokens, other, [[b_down], [b_up]], at(blocks_b(-1), blocks_b(1)), before=acc)
    a_down, a_up, acc = lax.optimization_barrier((a_down, a_up, acc))
    a_pass = halves([a_down, a_up], [0, 1])
    a_far = [shifted(a_pass[0], "z", 1), shifted(a_pass[1], "z", nz - 1)]
    by_x = turn(from_y, nx, d_rows)
    by_x, acc = lax.optimization_barrier((by_x, acc))
    from_x = exchange(by_x, "x")
    acc = add_blocks(tokens, other, [[a_down], [a_up]], at(blocks_a(-1), blocks_a(1)), before=acc)
    acc, from_x = lax.optimization_barrier((acc, from_x))
    tile, sent = add_blocks(tokens, other, [a_far, b_far], at(blocks_a(2), blocks_b(2)), before=acc, final=True)
    grad_down, grad_up, flags = finish(from_x, d_rows)
    back = lax.ppermute(sent, "c", SWAP)
    keys = jnp.concatenate([jnp.where(me_c == 0, tile, back), jnp.where(me_c == 0, back, tile)], axis=1)

    flag, keys = lax.optimization_barrier((flags[0, 0], keys))

    def again(state):
        first, down_sum, up_sum, _ = state
        _, theirs, mine, note = local_terms(first)
        by_owner = spread(exchange(pack(mine, lax.ppermute(theirs, "c", SWAP), note), "z"), owned_col, ny)
        by_x = turn(exchange(by_owner, "y"), nx, d_rows)
        down_more, up_more, flags = finish(exchange(by_x, "x"), d_rows)
        return first + SLOTS, down_sum + down_more, up_sum + up_more, flags[0, 0]

    _, grad_down, grad_up, _ = lax.while_loop(
        lambda state: state[3] > 0.5, again, (jnp.int32(SLOTS), grad_down, grad_up, flag)
    )
    return keys, grad_down[None], grad_up[None]


def solution(mesh):
    sizes = dict(mesh.shape)
    ny = sizes["grp"]
    nx = nz = int((sizes["fsdp"] // 2) ** 0.5)
    fine = Mesh(mesh.devices.reshape(ny, nx, nz, 2), ("y", "x", "z", "c"))
    fsdp = ("x", "z", "c")
    every = ("y", "x", "z", "c")
    in_specs = (P(every, None), P(fsdp, None), P(), P(), P(every, None), P(every), P(), P())
    out_specs = (P(every, None), P("y", fsdp, None), P("y", fsdp, None))
    return jax.shard_map(per_device, mesh=fine, in_specs=in_specs, out_specs=out_specs, check_vma=False)
```

```python
import jax
import jax.numpy as jnp
from jax import lax
from jax.experimental import pallas as pl
from jax.experimental.pallas import tpu as pltpu
from jax.sharding import Mesh, PartitionSpec as P

RANK = 64
SCALE = 0.5
BF = jnp.bfloat16
F32 = jnp.float32
SLOTS = 2
INFO = 16
MIB = 1 << 20
SWAP = [(0, 1), (1, 0)]


def dot(a, b, dims=((1,), (0,))):
    return lax.dot_general(a, b, (dims, ((), ())), preferred_element_type=F32)


def exchange(a, axis):
    return lax.all_to_all(a, axis, 0, 0, tiled=True)


def call(body, out, grid, in_specs, out_specs, scratch=(), flops=0, data=0, vmem=12):
    return pl.pallas_call(
        body,
        out_shape=out,
        grid=grid,
        in_specs=in_specs,
        out_specs=out_specs,
        scratch_shapes=list(scratch),
        compiler_params=pltpu.CompilerParams(vmem_limit_bytes=vmem * MIB),
        cost_estimate=pl.CostEstimate(flops=flops, bytes_accessed=data, transcendentals=0),
    )


def whole(shape):
    return pl.BlockSpec(shape, lambda *i: (0,) * len(shape))


def once(shape):
    return pl.BlockSpec(shape, lambda *i: (0,) * len(shape), pipeline_mode=pl.Buffered(1))


def terms(tokens, down, up, cotangent, tasks, token_weight, pick_t, col_task, v_from, me_c, nx, nz):
    n_tok, width = tokens.shape
    cols = down.shape[1]
    sc = pick_t.shape[0]
    kv = cotangent.shape[1]
    per = 4
    steps = nx * nz // per
    blk = width // steps
    d = width // (nx * nz * 2)
    half = kv // 2
    u = half // nz
    lanes = nx * d + u

    def body(me, tok, dn, up_ref, cot, task_col, task_row, tw, pick, picked, v_ref, hidden, theirs, mine, acc, sca, low):
        i = pl.program_id(0)
        first = me[0] == 0

        @pl.when(i == 0)
        def _():
            sca[...] = (cot[...].astype(F32) * tw[...]).astype(BF)
            up_slot = dot(pick[...], up_ref[...], ((1,), (1,))).astype(BF)
            g = dot(up_slot, sca[...], ((1,), (1,)))
            low[...] = jnp.where(picked[...] == task_row[...], g, 0.0).astype(BF)

        t = tok[...]
        part = dot(t, dn[...])

        @pl.when(i == 0)
        def _():
            acc[...] = part

        @pl.when(i > 0)
        def _():
            acc[...] += part

        r = dot(low[...], t).astype(BF)
        for k in range(per):
            x, z = (i * per + k) // nz, (i * per + k) % nz
            at = pl.ds(pl.multiple_of(x * d, d), d)
            a, b = r[:, 2 * k * d : (2 * k + 1) * d], r[:, (2 * k + 1) * d : (2 * k + 2) * d]
            mine[z, :, at] = jnp.where(first, a, b)
            theirs[z, :, at] = jnp.where(first, b, a)

        @pl.when(i == steps - 1)
        def _():
            adapter = lax.broadcasted_iota(jnp.int32, (n_tok, cols), 1) // RANK
            h = jnp.where(task_col[...] == adapter, acc[...], 0.0).astype(BF)
            hidden[...] = h
            h_t = dot(pick[...], h, ((1,), (1,))).astype(BF)
            order = lax.broadcasted_iota(jnp.int32, (kv, kv), 0) == v_ref[...]
            g = dot(dot(h_t, sca[...]).astype(BF), jnp.where(order, 1.0, 0.0).astype(BF)).astype(BF)
            for k in range(nz):
                a, b = g[:, k * u : (k + 1) * u], g[:, half + k * u : half + (k + 1) * u]
                mine[k, :, nx * d :] = jnp.where(first, a, b)
                theirs[k, :, nx * d :] = jnp.where(first, b, a)

    return call(
        body,
        (
            jax.ShapeDtypeStruct((n_tok, cols), BF),
            jax.ShapeDtypeStruct((nz, sc, lanes), BF),
            jax.ShapeDtypeStruct((nz, sc, lanes), BF),
        ),
        (steps,),
        [
            pl.BlockSpec(memory_space=pltpu.SMEM),
            pl.BlockSpec((n_tok, blk), lambda i: (0, i)),
            pl.BlockSpec((blk, cols), lambda i: (i, 0)),
            once((kv, cols)),
            once((n_tok, kv)),
            once((n_tok, 1)),
            once((1, n_tok)),
            once((n_tok, 1)),
            once((sc, cols)),
            once((sc, 1)),
            once((1, kv)),
        ],
        (whole((n_tok, cols)), whole((nz, sc, lanes)), whole((nz, sc, lanes))),
        [pltpu.VMEM((n_tok, cols), F32), pltpu.VMEM((n_tok, kv), BF), pltpu.VMEM((sc, n_tok), BF)],
        flops=2 * n_tok * width * (cols + sc),
        data=24 * MIB,
        vmem=28,
    )(
        me_c,
        tokens,
        down,
        up,
        cotangent,
        tasks[:, None],
        tasks[None, :],
        token_weight,
        pick_t,
        col_task[:, None],
        v_from[None, :],
    )


def join(*lists):
    n = len(lists[0])
    rows, lanes = lists[0][0].shape

    def body(*refs):
        for k in range(len(lists)):
            for j in range(n):
                refs[n * len(lists) + k][j * rows : (j + 1) * rows] = refs[k * n + j][...]

    return call(
        body,
        tuple(jax.ShapeDtypeStruct((n * rows, lanes), BF) for _ in lists),
        (1,),
        [once((rows, lanes))] * (n * len(lists)),
        tuple(whole((n * rows, lanes)) for _ in lists),
        data=4 * MIB,
    )(*[a for one in lists for a in one])


def halves(arrays, which):
    rows, lanes = arrays[0].shape
    steps = 2
    blk = rows // 2 // steps

    def body(*refs):
        for k in range(len(arrays)):
            refs[len(arrays) + k][...] = refs[k][...]

    return call(
        body,
        tuple(jax.ShapeDtypeStruct((rows // 2, lanes), BF) for _ in arrays),
        (steps,),
        [pl.BlockSpec((blk, lanes), lambda i, w=w: (w * steps + i, 0)) for w in which],
        tuple(pl.BlockSpec((blk, lanes), lambda i: (i, 0)) for _ in arrays),
        data=4 * MIB,
    )(*arrays)


def pack(mine, theirs, note):
    n, sc, lanes = mine.shape

    def body(a, b, c, out):
        out[0, :sc] = (a[0].astype(F32) + b[0].astype(F32)).astype(BF)
        out[0, sc:] = c[...]

    block = pl.BlockSpec((1, sc, lanes), lambda i: (i, 0, 0))
    return call(
        body,
        jax.ShapeDtypeStruct((n, sc + INFO, lanes), BF),
        (n,),
        [block, block, whole((INFO, lanes))],
        pl.BlockSpec((1, sc + INFO, lanes), lambda i: (i, 0, 0)),
        data=10 * MIB,
    )(mine, theirs, note)


def spread(got, owned_col, ny):
    n, rows, lanes = got.shape
    sc = rows - INFO
    cols = owned_col.shape[0]
    own = cols // ny

    def body(g, ow, out):
        total = jnp.zeros((own, lanes), F32)
        flag = jnp.zeros((1, lanes), BF)
        same = (
            lax.broadcasted_iota(jnp.int32, (own, sc), 0) % RANK
            == lax.broadcasted_iota(jnp.int32, (own, sc), 1) % RANK
        )
        for p in range(n):
            note = g[p, sc:, :]
            sent = note[0:1, :sc].astype(F32)
            place = jnp.where(same & (ow[...] == sent), 1.0, 0.0).astype(BF)
            total += dot(place, g[p, :sc, :])
            flag = jnp.maximum(flag, note[1:2, :])
        out[0, :own] = total.astype(BF)
        out[0, own:] = jnp.broadcast_to(flag, (INFO, lanes))

    return call(
        body,
        pltpu.HBM((ny, own + INFO, lanes), BF),
        (ny,),
        [once((n, rows, lanes)), pl.BlockSpec((own, 1), lambda i: (i, 0))],
        pl.BlockSpec((1, own + INFO, lanes), lambda i: (i, 0, 0)),
        flops=2 * cols * n * sc * lanes,
        data=5 * MIB,
    )(got, owned_col)


def turn(got, nx, d):
    n, rows, lanes = got.shape
    own = rows - INFO
    v = (lanes - nx * d) // nx

    def body(g, out):
        total = g[0, :own].astype(F32)
        flag = g[0, own : own + INFO, :own]
        for p in range(1, n):
            total += g[p, :own].astype(F32)
            flag = jnp.maximum(flag, g[p, own : own + INFO, :own])
        t = total.T.astype(BF)
        for x in range(nx):
            out[x, :d] = t[x * d : (x + 1) * d]
            out[x, d : d + v] = t[nx * d + x * v : nx * d + (x + 1) * v]
            out[x, d + v :] = flag

    return call(
        body,
        pltpu.HBM((nx, d + v + INFO, own), BF),
        (1,),
        [whole(got.shape)],
        whole((nx, d + v + INFO, own)),
        data=2 * MIB,
    )(got)


def finish(got, d):
    n, rows, own = got.shape
    v = rows - INFO - d

    def body(g, down, up, flag):
        total = g[0].astype(F32)
        most = g[0, d + v :].astype(F32)
        for p in range(1, n):
            total += g[p].astype(F32)
            most = jnp.maximum(most, g[p, d + v :].astype(F32))
        down[...] = total[:d]
        up[...] = total[d : d + v]
        flag[...] = most

    shapes = (d, own), (v, own), (INFO, own)
    return call(
        body,
        tuple(jax.ShapeDtypeStruct(s, F32) for s in shapes),
        (1,),
        [whole(got.shape)],
        tuple(whole(s) for s in shapes),
        data=MIB // 2,
    )(got)


def shifted(a, axis, step):
    n = lax.axis_size(axis)
    return lax.ppermute(a, axis, [(i, (i + step) % n) for i in range(n)])


def add_blocks(own, other, groups, where_from, before=None, lora=None, final=False):
    n_tok = own.shape[0]
    rows = sum(w.shape[0] for w in groups[0])
    n = groups[0][0].shape[1]
    steps = len(groups)
    per = where_from.shape[0] // steps
    blk = rows // per
    flat = [w for group in groups for w in group]
    extra = [] if before is None else [before]
    extra_specs = [once(e.shape) for e in extra]
    if lora is not None:
        extra += list(lora)
        extra_specs += [once(e.shape) for e in lora[:2]]
        extra_specs.append(pl.BlockSpec((n, lora[2].shape[1]), lambda i, s: (s[steps * per], 0)))

    def body(at, *refs):
        tok_a, tok_b = refs[:per], refs[per : 2 * per]
        ws = refs[2 * per : 2 * per + len(flat)]
        more = refs[2 * per + len(flat) : 2 * per + len(flat) + len(extra)]
        outs = refs[2 * per + len(flat) + len(extra) :]
        acc = refs[-1]
        i = pl.program_id(0)

        @pl.when(i == 0)
        def _():
            if before is not None:
                acc[...] = more[0][...]
            else:
                acc[...] = jnp.zeros_like(acc)
            if lora is not None:
                h_a, h_b, u = more[-3:]
                acc[:n_tok] += SCALE * dot(h_a[...], u[...], ((1,), (1,)))
                acc[n_tok:] += SCALE * dot(h_b[...], u[...], ((1,), (1,)))

        left = 0
        for p in range(steps):
            mine = ws[left : left + len(groups[p])]
            left += len(groups[p])

            @pl.when(i == p)
            def _(mine=mine):
                parts = [w[...] for w in mine]
                w = parts[0] if len(parts) == 1 else jnp.concatenate(parts, axis=0)
                acc[:n_tok] += dot(jnp.concatenate([t[...] for t in tok_a], axis=1), w)
                acc[n_tok:] += dot(jnp.concatenate([t[...] for t in tok_b], axis=1), w)

        if final:

            @pl.when(i == steps - 1)
            def _():
                outs[0][...] = acc[:n_tok].astype(BF)
                outs[1][...] = acc[n_tok:].astype(BF)

    tok_specs = [pl.BlockSpec((n_tok, blk), lambda i, s, k=k: (0, s[i * per + k])) for k in range(per)]
    shape = (2 * n_tok, n)
    return pl.pallas_call(
        body,
        out_shape=(jax.ShapeDtypeStruct((n_tok, n), BF),) * 2 if final else pltpu.HBM(shape, F32),
        grid_spec=pltpu.PrefetchScalarGridSpec(
            num_scalar_prefetch=1,
            grid=(steps,),
            in_specs=tok_specs * 2 + [once(w.shape) for w in flat] + extra_specs,
            out_specs=(whole((n_tok, n)),) * 2 if final else whole(shape),
            scratch_shapes=[pltpu.VMEM(shape, F32)] if final else [],
        ),
        compiler_params=pltpu.CompilerParams(vmem_limit_bytes=22 * MIB),
        cost_estimate=pl.CostEstimate(
            flops=4 * n_tok * rows * n * steps, bytes_accessed=8 * n_tok * rows * steps, transcendentals=0
        ),
    )(where_from, *([own] * per), *([other] * per), *flat, *extra)


def per_device(tokens, weight, down, up, cotangent, tasks, owned, counts):
    n_tok, width = tokens.shape
    kv = weight.shape[1]
    adapters = owned.shape[0]
    cols = adapters * RANK
    ny, nx, nz = lax.axis_size("y"), lax.axis_size("x"), lax.axis_size("z")
    me_c = lax.axis_index("c")
    d_rows, v_rows = width // (nx * nz * 2), kv // (nx * nz * 2)
    me_x, me_z = lax.axis_index("x"), lax.axis_index("z")
    sc = SLOTS * RANK
    lanes = nx * (d_rows + v_rows)
    half = kv // 2

    def columns(a, core):
        return lax.dynamic_slice_in_dim(a, core * half, half, 1)

    block_a = columns(weight, me_c)
    block_b = lax.ppermute(columns(weight, 1 - me_c), "c", SWAP)
    partner_tasks = lax.ppermute(tasks, "c", SWAP)
    block_b, partner_tasks, cotangent, counts = lax.optimization_barrier((block_b, partner_tasks, cotangent, counts))
    first_hop = [shifted(block_a, "x", k) for k in range(1, nx)] + [shifted(block_b, "z", k) for k in range(1, nz)]
    def blocks_a(step):
        z = (me_z + step) % nz
        return [(((me_x - k) % nx) * nz + z) * 2 + me_c for k in range(nx)]

    def blocks_b(step):
        x = (me_x + step) % nx
        return [(x * nz + (me_z - k) % nz) * 2 + 1 - me_c for k in range(nz)]

    def at(*lists):
        return jnp.stack([i for one in lists for i in one]).astype(jnp.int32)

    ids = jnp.arange(adapters, dtype=jnp.int32)
    hit = tasks[:, None] == ids[None, :]
    present = jnp.any(hit | (partner_tasks[:, None] == ids[None, :]), axis=0)
    rank_of = jnp.sum((ids[None, :] < ids[:, None]) & present[None, :], axis=1)
    col_slot = jnp.arange(sc, dtype=jnp.int32) // RANK
    col_rank = jnp.arange(sc, dtype=jnp.int32) % RANK
    row = jnp.arange(cols, dtype=jnp.int32)

    token_count = jnp.sum(jnp.where(hit, counts.astype(F32)[None, :], 0.0), axis=1)
    token_weight = (SCALE / token_count)[:, None]
    v_out = jnp.arange(kv, dtype=jnp.int32)
    v_from = (
        (v_out // v_rows % nx) * (nz * 2 * v_rows)
        + (v_out // (v_rows * nx) % nz) * (2 * v_rows)
        + v_out // (v_rows * nx * nz) * v_rows
        + v_out % v_rows
    )

    owned_col = jnp.repeat(owned.astype(F32), RANK)[:, None]

    def local_terms(first):
        chosen = present[None, :] & (rank_of[None, :] == first + col_slot[:, None])
        col_task = jnp.sum(jnp.where(chosen, ids[None, :] + 1, 0), axis=1) - 1
        more = (jnp.sum(present.astype(jnp.int32)) > first + SLOTS).astype(F32)
        pick_t = ((row // RANK)[None, :] == col_task[:, None]) & ((row % RANK)[None, :] == col_rank[:, None])
        pick_t = pick_t.astype(BF)
        hidden, theirs, mine = terms(
            tokens,
            down,
            up,
            cotangent,
            tasks,
            token_weight,
            pick_t,
            col_task,
            v_from,
            me_c.astype(jnp.int32)[None],
            nx,
            nz,
        )
        note_row = lax.broadcasted_iota(jnp.int32, (INFO, lanes), 0)
        note = jnp.where(note_row == 0, jnp.pad(col_task.astype(F32), (0, lanes - sc))[None, :], more)
        return hidden, theirs, mine, note.astype(BF)

    hidden, theirs, mine, note = local_terms(jnp.int32(0))
    first_hop, theirs = lax.optimization_barrier((first_hop, theirs))
    near_a, near_b = join([block_a] + first_hop[: nx - 1], [block_b] + first_hop[nx - 1 :])
    near_a, near_b, theirs, sent_hidden = lax.optimization_barrier((near_a, near_b, theirs, hidden))
    got = lax.ppermute(theirs, "c", SWAP)
    other_hidden = lax.ppermute(sent_hidden, "c", SWAP)
    chip = pack(mine, got, note)
    sent_tokens, _ = lax.optimization_barrier((tokens, got))
    other = lax.ppermute(sent_tokens, "c", SWAP)
    near_a, other, _ = lax.optimization_barrier((near_a, other, chip))
    a_down, a_up = shifted(near_a, "z", 1), shifted(near_a, "z", nz - 1)
    b_down, b_up = shifted(near_b, "x", 1), shifted(near_b, "x", nx - 1)
    from_z = exchange(chip, "z")

    acc = add_blocks(
        tokens,
        other,
        [[near_a], [near_b]],
        at(blocks_a(0), blocks_b(0), [me_c]),
        lora=(hidden, other_hidden, up),
    )
    from_z, acc = lax.optimization_barrier((from_z, acc))
    b_down, b_up, _ = lax.optimization_barrier((b_down, b_up, from_z))
    from_y = exchange(spread(from_z, owned_col, ny), "y")
    b_pass = halves([b_down, b_up], [0, 1])
    b_far = [shifted(b_pass[0], "x", 1), shifted(b_pass[1], "x", nx - 1)]
    acc = add_blocks(tokens, other, [[b_down], [b_up]], at(blocks_b(-1), blocks_b(1)), before=acc)
    a_down, a_up, acc = lax.optimization_barrier((a_down, a_up, acc))
    a_pass = halves([a_down, a_up], [0, 1])
    a_far = [shifted(a_pass[0], "z", 1), shifted(a_pass[1], "z", nz - 1)]
    by_x = turn(from_y, nx, d_rows)
    by_x, acc = lax.optimization_barrier((by_x, acc))
    from_x = exchange(by_x, "x")
    acc = add_blocks(tokens, other, [[a_down], [a_up]], at(blocks_a(-1), blocks_a(1)), before=acc)
    acc, from_x = lax.optimization_barrier((acc, from_x))
    tile, sent = add_blocks(tokens, other, [[w] for w in a_far + b_far], at(blocks_a(2), blocks_b(2)), before=acc, final=True)
    grad_down, grad_up, flags = finish(from_x, d_rows)
    back = lax.ppermute(sent, "c", SWAP)
    keys = jnp.concatenate([jnp.where(me_c == 0, tile, back), jnp.where(me_c == 0, back, tile)], axis=1)

    flag, keys = lax.optimization_barrier((flags[0, 0], keys))

    def again(state):
        first, down_sum, up_sum, _ = state
        _, theirs, mine, note = local_terms(first)
        by_owner = spread(exchange(pack(mine, lax.ppermute(theirs, "c", SWAP), note), "z"), owned_col, ny)
        by_x = turn(exchange(by_owner, "y"), nx, d_rows)
        down_more, up_more, flags = finish(exchange(by_x, "x"), d_rows)
        return first + SLOTS, down_sum + down_more, up_sum + up_more, flags[0, 0]

    _, grad_down, grad_up, _ = lax.while_loop(
        lambda state: state[3] > 0.5, again, (jnp.int32(SLOTS), grad_down, grad_up, flag)
    )
    return keys, grad_down[None], grad_up[None]


def solution(mesh):
    sizes = dict(mesh.shape)
    ny = sizes["grp"]
    nx = nz = int((sizes["fsdp"] // 2) ** 0.5)
    fine = Mesh(mesh.devices.reshape(ny, nx, nz, 2), ("y", "x", "z", "c"))
    fsdp = ("x", "z", "c")
    every = ("y", "x", "z", "c")
    in_specs = (P(every, None), P(fsdp, None), P(), P(), P(every, None), P(every), P(), P())
    out_specs = (P(every, None), P("y", fsdp, None), P("y", fsdp, None))
    return jax.shard_map(per_device, mesh=fine, in_specs=in_specs, out_specs=out_specs, check_vma=False)
```
